32 devices in a mesh: gx: 4 (over z), gy: 2 (over y), rep: 4 (over x, core).
Axes of the slice: x: 2, y: 2, z: 4, core: 2. Of those that a mesh axis runs over, the one named last changes fastest.
Arguments:
- positions: float32 [4, 3, 64, 4096], P('rep', None, 'gx', 'gy'), may hold values from 0 to 4
- velocities: float32 [4, 3, 64, 4096], P('rep', None, 'gx', 'gy'), may hold values from -6 to 6
- noise: float32 [4, 3, 64, 4096], P('rep', None, 'gx', 'gy'), may hold values from -6 to 6
- bonds: int32 [64, 64, 8], P('gx', 'gy'), may hold values from 0 to 1, as said below
Outputs:
- mean_force: float32 [3, 64, 4096], P(None, 'gx', 'gy')
- new_velocity: float32 [4, 3, 64, 4096], P('rep', None, 'gx', 'gy')
- new_position: float32 [4, 3, 64, 4096], P('rep', None, 'gx', 'gy')
The draws below stay inside these ranges and needn't reach their ends.
Inputs may be any that keep to these rules, and one draw needn't show every extreme that they name: bonds is symmetric: bonds of cluster c for offset k equals bonds of cluster c + offset k for the opposite offset k + 4 (k < 4); entries for neighbours outside the grid are 0.
All inputs are finite; a program needn't handle non-finite values.
Results may differ from the reference program's by a relative error of at most 0.0001.
Values sent between devices are 32-bit elements; how exact they have to be, the bound alone decides.
A program may use at most 64 MiB of HBM per device.

```python
import jax
import jax.numpy as jnp
from jax import lax

ATOMS = 64
NXC = 64
NYC = 64
REPS = 4
N_REP = 4


half_offsets = ((0, 1), (1, -1), (1, 0), (1, 1))


def draw_bonds(key, part):
    half_flags = (jax.random.randint(key, (NXC, NYC, 4), 0, 4) < 3).astype(jnp.int32)
    row_ids = jnp.arange(NXC, dtype=jnp.int32)[:, None]
    col_ids = jnp.arange(NYC, dtype=jnp.int32)[None, :]
    forward = []
    for offset_index in range(4):
        shift_x, shift_y = half_offsets[offset_index]
        inside = (row_ids + shift_x >= 0) & (row_ids + shift_x < NXC) & (col_ids + shift_y >= 0) & (col_ids + shift_y < NYC)
        forward.append(half_flags[:, :, offset_index] * inside.astype(jnp.int32))
    forward_flags = jnp.stack(forward, axis=-1)
    padded = jnp.pad(forward_flags, ((1, 1), (1, 1), (0, 0)))
    backward = []
    for offset_index in range(4):
        shift_x, shift_y = half_offsets[offset_index]
        backward.append(padded[1 - shift_x:1 - shift_x + NXC, 1 - shift_y:1 - shift_y + NYC, offset_index])
    return jnp.concatenate([forward_flags, jnp.stack(backward, axis=-1)], axis=-1).astype(jnp.int32)


def levels(rng, shape, pieces, smallest, largest):
    gain, own = 1.0, jax.random.fold_in(rng, 6)
    for axis_at, blocks in pieces:
        heights = jnp.exp(jax.random.uniform(jax.random.fold_in(own, axis_at), (blocks,), jnp.float32, smallest / len(pieces), largest / len(pieces)))
        gain = gain * jnp.repeat(heights, shape[axis_at] // blocks).reshape([-1 if axis == axis_at else 1 for axis in range(len(shape))])
    return gain


def bell_draw(key, dims, spread, limit, cuts=(), kind=jnp.bfloat16):
    values = jax.random.normal(key, dims, jnp.float32) * spread
    if len(cuts) > 0:
        values = levels(key, dims, cuts, -0.22, 0.18) * values
    return jnp.clip(values, min=-limit, max=limit).astype(kind)


def setup_inputs(seed: int = 0) -> dict:
    splits = jax.random.split(jax.random.key(seed), 5)
    return {
        "positions": jnp.clip(4.0 * jax.random.uniform(splits[0], (REPS, 3, NXC, NYC * ATOMS), jnp.float32) ** levels(splits[0], (REPS, 3, NXC, NYC * ATOMS), ((0, 4), (2, 4), (3, 2)), -0.2, 0.2), 0.0, 4.0),
        "velocities": bell_draw(splits[1], (REPS, 3, NXC, NYC * ATOMS), 1.0, 6.0, ((0, 4), (2, 4), (3, 2)), jnp.float32),
        "noise": bell_draw(splits[2], (REPS, 3, NXC, NYC * ATOMS), 1.0, 6.0, ((0, 4), (2, 4), (3, 2)), jnp.float32),
        "bonds": draw_bonds(jax.random.fold_in(splits[4], 71), 0),
    }


spacing = 4.0
friction = 0.6
noise_coef = 0.8
time_step = 0.2
offsets_list = ((0, 1), (1, -1), (1, 0), (1, 1), (0, -1), (-1, 1), (-1, 0), (-1, -1))


def pair_weight(squared):
    return 2.0 * jnp.exp(-2.0 * squared) - 0.5 * jnp.exp(-0.5 * squared)


def tile_forces(own_atoms, neighbour, flag_col, shift_x, shift_y):
    shift_vec = jnp.array([shift_x * spacing, shift_y * spacing, 0.0], jnp.float32)[:, None, None]
    moved_atoms = neighbour + shift_vec
    differ = own_atoms[:, :, :, None] - moved_atoms[:, :, None, :]
    squared = jnp.sum(differ * differ, axis=0)
    weighted = (pair_weight(squared) * flag_col[:, None, None])[None] * differ
    return jnp.sum(weighted, axis=3), -jnp.sum(weighted, axis=2)


def reference(positions, velocities, noise, bonds):
    rows_total = positions.shape[2]
    cols_total = positions.shape[3] // ATOMS
    cluster_grid = positions.reshape(positions.shape[0], 3, rows_total, cols_total, ATOMS)
    padded = jnp.pad(cluster_grid, ((0, 0), (0, 0), (1, 1), (1, 1), (0, 0)))
    flag_all = bonds.astype(jnp.float32)
    ones_flag = jnp.ones((cols_total,), jnp.float32)

    def replica_force(padded_rep):
        def row_force(row_index):
            window = lax.dynamic_slice_in_dim(padded_rep, row_index, 3, 1)
            own_atoms = window[:, 1, 1:cols_total + 1]
            flag_row = lax.dynamic_index_in_dim(flag_all, row_index, 0, keepdims=False)
            summed = tile_forces(own_atoms, own_atoms, ones_flag, 0, 0)[0]
            for offset_index, (shift_x, shift_y) in enumerate(offsets_list):
                neighbour = window[:, 1 + shift_x, 1 + shift_y:1 + shift_y + cols_total]
                summed = summed + tile_forces(own_atoms, neighbour, flag_row[:, offset_index], shift_x, shift_y)[0]
            return summed

        return lax.map(row_force, jnp.arange(rows_total, dtype=jnp.int32))

    forces = lax.map(replica_force, padded)
    averaged = jnp.sum(forces, axis=0) / N_REP
    mean_force = jnp.transpose(averaged, (1, 0, 2, 3)).reshape(3, rows_total, cols_total * ATOMS)
    new_velocity = friction * velocities + time_step * mean_force[None] + noise_coef * noise
    new_position = positions + time_step * new_velocity
    return mean_force, new_velocity, new_position
```

```python
import jax
import jax.numpy as jnp
from jax import lax
from jax.experimental import pallas as pl
from jax.experimental.pallas import tpu as pltpu
from jax.sharding import PartitionSpec as P

ATOMS = 64
TILE = 128

spacing = 4.0
friction = 0.6
noise_coef = 0.8
time_step = 0.2
centre = 2.0
alpha = 0.5 * 1.4426950408889634
ratio = 4.0 ** (-1.0 / 3.0)
blocked = -16384.0
offset_at = ((7, 6, 5), (4, -1, 0), (1, 2, 3))


def passed_along(value, axis, steps):
    count = lax.axis_size(axis)
    leading, last = (max(0, -steps), min(count, count - steps))
    return lax.ppermute(value, axis, [(source, source + steps) for source in range(leading, last)])


def iota(shape, axis):
    return lax.broadcasted_iota(jnp.int32, shape, axis)


def split3(value):
    first = value.astype(jnp.bfloat16).astype(jnp.float32)
    rest = value - first
    second = rest.astype(jnp.bfloat16).astype(jnp.float32)
    return first, second, rest - second


def force_kernel(ext_ref, pos_ref, bias_ref, out_ref, lhs_ref, coef_ref, rhs_ref, shifted_ref):
    rows_ext, _, wide = ext_ref.shape
    rows_local, _, lanes = pos_ref.shape
    cols_local = lanes // ATOMS
    tiles = lanes // TILE

    def neighbour_features(row, carry):
        sub = iota((8, wide), 0)
        slot = iota((8, wide), 1) // ATOMS
        base = ext_ref[row] - centre
        stacked = []
        for parity in range(2):
            role = lax.rem(slot + 2 * parity, 4)
            moved = base + jnp.where(sub == 1, (role.astype(jnp.float32) - 1.5) * spacing, 0.0)
            moved = jnp.where(sub < 3, moved, 0.0)
            square = -alpha * jnp.sum(moved * moved, axis=0, keepdims=True)
            vec = jnp.where(sub == 3, square, jnp.where(sub == 4, 1.0, moved))
            one, two, three = split3(vec)
            hot = jnp.where(sub == role, 1.0, 0.0)
            zero = jnp.zeros_like(hot)
            stacked += [one, one, one, two, two, three, hot, zero]
            coef_ref[row, parity] = jnp.concatenate([one, two, three, zero], axis=0).astype(jnp.bfloat16)
        whole = jnp.concatenate(stacked, axis=0)
        for t in range(wide // TILE):
            lhs_ref[row, t * TILE : (t + 1) * TILE] = whole[:, t * TILE : (t + 1) * TILE].T.astype(jnp.bfloat16)
        return carry

    lax.fori_loop(0, rows_ext, neighbour_features, 0)

    def own_row(row, carry):
        sub = iota((8, lanes), 0)
        half = lax.rem(iota((8, lanes), 1) // ATOMS, 2).astype(jnp.float32)
        expand = (iota((cols_local, lanes), 1) // ATOMS == iota((cols_local, lanes), 0)).astype(jnp.bfloat16)
        bias = jnp.dot(bias_ref[row].astype(jnp.bfloat16), expand, preferred_element_type=jnp.float32)
        base = pos_ref[row] - centre
        base = base + jnp.where(sub == 1, (half - 0.5) * spacing, 0.0)
        for step in range(3):
            moved = base - jnp.where(sub == 0, (step - 1) * spacing, 0.0)
            moved = jnp.where(sub < 3, moved, 0.0)
            shifted_ref[step] = moved
            square = 2.0 / 3.0 - alpha * jnp.sum(moved * moved, axis=0, keepdims=True)
            vec = jnp.where(sub == 3, 1.0, jnp.where(sub == 4, square, 2.0 * alpha * moved))
            one, two, three = split3(vec)
            flags = bias[8 * step : 8 * step + 8]
            rhs_ref[step] = jnp.concatenate(
                [one, two, three, one, two, one, flags, jnp.zeros_like(flags)], axis=0
            ).astype(jnp.bfloat16)

        def tile_pair(pair, inner):
            for parity in range(2):
                start = pl.multiple_of((2 * pair + parity) * TILE, TILE)
                total = jnp.zeros((8, TILE), jnp.float32)
                for step in range(3):
                    feat = rhs_ref[step, :, pl.ds(start, TILE)]
                    none = jnp.zeros_like(feat)
                    rhs = jnp.concatenate([feat, none] if parity == 0 else [none, feat], axis=0)
                    lhs = lhs_ref[row + step, pl.ds(start, 2 * TILE)]
                    power = jnp.dot(lhs, rhs, preferred_element_type=jnp.float32)
                    soft = jnp.exp2(power)
                    square = soft * soft
                    weight = square * square - soft
                    high = weight.astype(jnp.bfloat16)
                    low = (weight - high.astype(jnp.float32)).astype(jnp.bfloat16)
                    both = jnp.concatenate([high, low], axis=1)
                    coef = coef_ref[row + step, parity, :, pl.ds(start, 2 * TILE)]
                    sums = jnp.dot(coef, both, preferred_element_type=jnp.float32)
                    sums = sums[:, :TILE] + sums[:, TILE:]
                    sums = sums[0:8] + sums[8:16] + sums[16:24]
                    total = total + shifted_ref[step, :, pl.ds(start, TILE)] * sums[4:5] - sums
                out_ref[row, :, pl.ds(start, TILE)] = (0.5 * ratio) * total
            return inner

        lax.fori_loop(0, tiles // 2, tile_pair, 0)
        return carry

    lax.fori_loop(0, rows_local, own_row, 0)


def cluster_forces(ext, pos, bias):
    rows_ext, _, wide = ext.shape
    rows_local, _, lanes = pos.shape
    return pl.pallas_call(
        force_kernel,
        out_shape=jax.ShapeDtypeStruct((rows_local, 8, lanes), jnp.float32),
        in_specs=[pl.BlockSpec(memory_space=pltpu.VMEM)] * 3,
        out_specs=pl.BlockSpec(memory_space=pltpu.VMEM),
        scratch_shapes=[
            pltpu.VMEM((rows_ext, wide, TILE), jnp.bfloat16),
            pltpu.VMEM((rows_ext, 2, 32, wide), jnp.bfloat16),
            pltpu.VMEM((3, 64, lanes), jnp.bfloat16),
            pltpu.VMEM((3, 8, lanes), jnp.float32),
        ],
        compiler_params=pltpu.CompilerParams(vmem_limit_bytes=40 * 1024 * 1024),
        name="cluster_forces",
    )(ext, pos, bias)


def bond_bias(bonds):
    cols_local = bonds.shape[1]
    odd = (jnp.arange(cols_local) % 2 == 1)[None, :]
    rows = []
    for step in range(3):
        flags = [
            jnp.ones(bonds.shape[:2], bonds.dtype) if k < 0 else bonds[:, :, k] for k in offset_at[step]
        ]
        none = jnp.zeros_like(flags[0])
        for role in range(8):
            even_flag = flags[role] if role < 3 else none
            odd_flag = flags[role - 1] if 1 <= role < 4 else none
            rows.append(jnp.where(odd, odd_flag, even_flag))
    picked = jnp.stack(rows, axis=1)
    return jnp.where(picked != 0, 0.0, blocked).astype(jnp.float32)


def per_device(positions, velocities, noise, bonds):
    rows_local = positions.shape[2]
    lanes = positions.shape[3]
    coords = positions[0]
    lower = passed_along(coords[:, :, lanes - ATOMS :], "gy", 1)
    upper = passed_along(coords[:, :, :ATOMS], "gy", -1)
    widened = jnp.concatenate([lower, coords, upper], axis=2)
    before = passed_along(widened[:, rows_local - 1 :], "gx", 1)
    after = passed_along(widened[:, :1], "gx", -1)
    ext = jnp.concatenate([before, widened, after], axis=1)
    ext = jnp.pad(jnp.transpose(ext, (1, 0, 2)), ((0, 0), (0, 5), (0, 0)))
    own = jnp.pad(jnp.transpose(coords, (1, 0, 2)), ((0, 0), (0, 5), (0, 0)))
    forces = cluster_forces(ext, own, bond_bias(bonds))
    own_force = jnp.transpose(forces[:, :3], (1, 0, 2))
    mean_force = lax.psum(own_force, "rep") / lax.axis_size("rep")
    new_velocity = friction * velocities + time_step * mean_force[None] + noise_coef * noise
    new_position = positions + time_step * new_velocity
    return (mean_force, new_velocity, new_position)


def solution(mesh):
    in_specs = (
        P("rep", None, "gx", "gy"),
        P("rep", None, "gx", "gy"),
        P("rep", None, "gx", "gy"),
        P("gx", "gy", None),
    )
    out_specs = (P(None, "gx", "gy"), P("rep", None, "gx", "gy"), P("rep", None, "gx", "gy"))
    return jax.shard_map(
        per_device, mesh=mesh, in_specs=in_specs, out_specs=out_specs, check_vma=False
    )
```

```python
import jax
import jax.numpy as jnp
from jax import lax
from jax.experimental import pallas as pl
from jax.experimental.pallas import tpu as pltpu
from jax.sharding import PartitionSpec as P

ATOMS = 64
TILE = 128

spacing = 4.0
friction = 0.6
noise_coef = 0.8
time_step = 0.2
centre = 2.0
alpha = 0.5 * 1.4426950408889634
ratio = 4.0 ** (-1.0 / 3.0)
blocked = -16384.0
offset_at = ((7, 6, 5), (4, -1, 0), (1, 2, 3))


def iota(shape, axis):
    return lax.broadcasted_iota(jnp.int32, shape, axis)


def split3(value):
    first = value.astype(jnp.bfloat16).astype(jnp.float32)
    rest = value - first
    second = rest.astype(jnp.bfloat16).astype(jnp.float32)
    return first, second, rest - second


directions = ((-1, -1), (-1, 0), (-1, 1), (0, -1), (0, 1), (1, -1), (1, 0), (1, 1))
MESH = pl.DeviceIdType.MESH


def row_of(ref, row):
    sub = iota((8, ref.shape[2]), 0)
    pieces = [ref[d, pl.ds(row, 1), :] for d in range(3)]
    return jnp.where(sub == 0, pieces[0], jnp.where(sub == 1, pieces[1], jnp.where(sub == 2, pieces[2], 0.0)))


def step_kernel(
    pos_ref, vel_ref, noise_ref, bias_ref,
    mean_ref, new_vel_ref, new_pos_ref,
    lhs_ref, coef_ref, rhs_ref, base_ref, slot_ref, stage_ref, row_ref, col_ref, hold_ref,
    halo_send, halo_recv, rep_send, rep_recv,
):
    _, rows_local, lanes = pos_ref.shape
    cols_local = lanes // ATOMS
    tiles = lanes // TILE
    wide = lanes + TILE
    pairs = tiles // 2
    groups = rows_local // 8
    gx, gy, rep = lax.axis_index("gx"), lax.axis_index("gy"), lax.axis_index("rep")
    n_gx, n_gy, n_rep = lax.axis_size("gx"), lax.axis_size("gy"), lax.axis_size("rep")

    def present(dx, dy):
        checks = []
        if dx < 0:
            checks.append(gx > 0)
        if dx > 0:
            checks.append(gx < n_gx - 1)
        if dy < 0:
            checks.append(gy > 0)
        if dy > 0:
            checks.append(gy < n_gy - 1)
        found = checks[0]
        for check in checks[1:]:
            found = found & check
        return found

    barrier = pltpu.get_barrier_semaphore()
    expected = jnp.int32(n_rep - 1)
    for dx, dy in directions:
        there = present(dx, dy)
        expected = expected + there.astype(jnp.int32)

        @pl.when(there)
        def _():
            pl.semaphore_signal(barrier, inc=1, device_id={"gx": gx + dx, "gy": gy + dy}, device_id_type=MESH)

    for hop in range(1, n_rep):
        pl.semaphore_signal(barrier, inc=1, device_id={"rep": lax.rem(rep + hop, n_rep)}, device_id_type=MESH)

    stage_ref[0] = row_of(pos_ref, 0)
    stage_ref[1] = row_of(pos_ref, rows_local - 1)

    def halo_place(dx, dy):
        side = 0 if dx > 0 else 1
        if dx == 0:
            source = pos_ref.at[:, :, pl.ds(lanes - TILE if dy > 0 else 0, TILE)]
            return source, col_ref.at[0 if dy > 0 else 1]
        if dy == 0:
            return stage_ref.at[1 if dx > 0 else 0], row_ref.at[side, :, pl.ds(TILE, lanes)]
        source = stage_ref.at[1 if dx > 0 else 0, :, pl.ds(lanes - TILE if dy > 0 else 0, TILE)]
        return source, row_ref.at[side, :, pl.ds(0 if dy > 0 else TILE + lanes, TILE)]

    def halo_copy(k):
        dx, dy = directions[k]
        source, target = halo_place(dx, dy)
        return pltpu.make_async_remote_copy(
            src_ref=source, dst_ref=target, send_sem=halo_send.at[k], recv_sem=halo_recv.at[k],
            device_id={"gx": gx + dx, "gy": gy + dy}, device_id_type=MESH,
        )

    pl.semaphore_wait(barrier, expected)
    for k, (dx, dy) in enumerate(directions):
        @pl.when(present(dx, dy))
        def _():
            halo_copy(k).start()

    def own_row(row, carry):
        sub = iota((8, lanes), 0)
        half = lax.rem(iota((8, lanes), 1) // ATOMS, 2).astype(jnp.float32)
        expand = (iota((cols_local, lanes), 1) // ATOMS == iota((cols_local, lanes), 0)).astype(jnp.bfloat16)
        bias = jnp.dot(bias_ref[row].astype(jnp.bfloat16), expand, preferred_element_type=jnp.float32)
        base = row_of(pos_ref, row) - centre
        base = base + jnp.where(sub == 1, (half - 0.5) * spacing, 0.0)
        base_ref[row] = base
        for step in range(3):
            moved = base - jnp.where(sub == 0, (step - 1) * spacing, 0.0)
            moved = jnp.where(sub < 3, moved, 0.0)
            square = 2.0 / 3.0 - alpha * jnp.sum(moved * moved, axis=0, keepdims=True)
            vec = jnp.where(sub == 3, 1.0, jnp.where(sub == 4, square, 2.0 * alpha * moved))
            one, two, three = split3(vec)
            flags = bias[8 * step : 8 * step + 8]
            rhs_ref[row, step] = jnp.concatenate(
                [one, two, three, one, two, one, flags, jnp.zeros_like(flags)], axis=0
            ).astype(jnp.bfloat16)
        return carry

    lax.fori_loop(0, rows_local, own_row, 0)

    for k, (dx, dy) in enumerate(directions):
        @pl.when(present(-dx, -dy))
        def _():
            halo_copy(k).wait_recv()

        @pl.when(jnp.logical_not(present(-dx, -dy)))
        def _():
            target = halo_place(dx, dy)[1]
            target[...] = jnp.zeros(target.shape, jnp.float32)

    def features(row, whole_row):
        sub = iota((8, wide), 0)
        slot = iota((8, wide), 1) // ATOMS
        base = pltpu.roll(whole_row, wide + TILE - ATOMS, 1)[:, :wide] - centre
        stacked = []
        for parity in range(2):
            role = lax.rem(slot + 2 * parity, 4)
            moved = base + jnp.where(sub == 1, (role.astype(jnp.float32) - 1.5) * spacing, 0.0)
            moved = jnp.where(sub < 3, moved, 0.0)
            square = -alpha * jnp.sum(moved * moved, axis=0, keepdims=True)
            vec = jnp.where(sub == 3, square, jnp.where(sub == 4, 1.0, moved))
            one, two, three = split3(vec)
            hot = jnp.where(sub == role, 1.0, 0.0)
            stacked += [one, one, one, two, two, three, hot, jnp.zeros_like(hot)]
            coef_ref[row, parity] = jnp.concatenate([one, two], axis=0).astype(jnp.bfloat16)
        whole = jnp.concatenate(stacked, axis=0)
        for t in range(wide // TILE):
            lhs_ref[row, t * TILE : (t + 1) * TILE] = whole[:, t * TILE : (t + 1) * TILE].T.astype(jnp.bfloat16)

    def inner_features(row, carry):
        features(row + 1, jnp.concatenate([row_of(col_ref.at[0], row), row_of(pos_ref, row), row_of(col_ref.at[1], row)], axis=1))
        return carry

    lax.fori_loop(0, rows_local, inner_features, 0)
    features(0, row_ref[0])
    features(rows_local + 1, row_ref[1])

    def weights(lhs, rhs):
        soft = jnp.exp2(jnp.dot(lhs, rhs, preferred_element_type=jnp.float32))
        square = soft * soft
        weight = square * square - soft
        high = weight.astype(jnp.bfloat16)
        return high, (weight - high.astype(jnp.float32)).astype(jnp.bfloat16)

    def rep_copy(hop, group, pair):
        chunk = slot_ref.at[
            rep, :, pl.ds(pl.multiple_of(group * 8, 8), 8), pl.ds(pl.multiple_of(pair * 2 * TILE, 2 * TILE), 2 * TILE)
        ]
        return pltpu.make_async_remote_copy(
            src_ref=chunk, dst_ref=chunk,
            send_sem=rep_send.at[hop - 1, group * pairs + pair], recv_sem=rep_recv.at[hop - 1, group * pairs + pair],
            device_id={"rep": lax.rem(rep + hop, n_rep)}, device_id_type=MESH,
        )

    def tile_rows(row, place, start, parity):
        lanes_at = pl.ds(start, TILE)
        shifts = [jnp.where(iota((8, TILE), 0) == 0, (step - 1) * spacing, 0.0) for step in range(3)]
        bases = [base_ref[row + r, :, lanes_at] for r in range(2)]
        totals = [jnp.zeros((8, TILE), jnp.float32) for _ in range(2)]

        def feat(r, step):
            block = rhs_ref[row + r, step, :, lanes_at]
            none = jnp.zeros_like(block)
            return jnp.concatenate([block, none] if parity == 0 else [none, block], axis=0)

        for q in range(4):
            lhs = lhs_ref[row + q, pl.ds(start, 2 * TILE)]
            coef = coef_ref[row + q, parity, :, pl.ds(start, 2 * TILE)]
            served = [(r, q - r) for r in range(2) if 0 <= q - r < 3]
            rhs = jnp.concatenate([feat(r, step) for r, step in served], axis=1)
            high, low = weights(lhs, rhs)
            if len(served) == 1:
                sums = jnp.dot(coef, jnp.concatenate([high, low], axis=1), preferred_element_type=jnp.float32)
                sums = sums[:, :TILE] + sums[:, TILE:]
            else:
                sums = jnp.dot(coef, high, preferred_element_type=jnp.float32)
                sums = sums + jnp.dot(coef, low, preferred_element_type=jnp.float32)
            sums = sums[0:8] + sums[8:16]
            for at, (r, step) in enumerate(served):
                part = sums[:, at * TILE : (at + 1) * TILE]
                totals[r] = totals[r] + (bases[r] - shifts[step]) * part[4:5] - part
        for r in range(2):
            hold_ref[place + r, :, parity * TILE : (parity + 1) * TILE] = (0.5 * ratio) * totals[r]

    def chunk_step(at, carry):
        group, pair = at // pairs, lax.rem(at, pairs)

        def row_pair(inner, unused):
            for parity in range(2):
                start = pl.multiple_of((2 * pair + parity) * TILE, TILE)
                tile_rows(group * 8 + inner * 2, inner * 2, start, parity)
            return unused

        lax.fori_loop(0, 4, row_pair, 0)
        sub = iota((8, 2 * TILE), 0)
        for d in range(3):
            block = jnp.zeros((8, 2 * TILE), jnp.float32)
            for r in range(8):
                block = jnp.where(sub == r, hold_ref[r, d : d + 1], block)
            slot_ref[
                rep, d, pl.ds(pl.multiple_of(group * 8, 8), 8), pl.ds(pl.multiple_of(pair * 2 * TILE, 2 * TILE), 2 * TILE)
            ] = block
        for hop in range(1, n_rep):
            rep_copy(hop, group, pair).start()
        return carry

    lax.fori_loop(0, groups * pairs, chunk_step, 0)

    def finish(at, carry):
        group, pair = at // pairs, lax.rem(at, pairs)
        for hop in range(1, n_rep):
            chunk = slot_ref.at[
                lax.rem(rep + n_rep - hop, n_rep), :,
                pl.ds(pl.multiple_of(group * 8, 8), 8), pl.ds(pl.multiple_of(pair * 2 * TILE, 2 * TILE), 2 * TILE),
            ]
            pltpu.make_async_remote_copy(
                src_ref=chunk, dst_ref=chunk,
                send_sem=rep_send.at[hop - 1, at], recv_sem=rep_recv.at[hop - 1, at],
                device_id={"rep": lax.rem(rep + hop, n_rep)}, device_id_type=MESH,
            ).wait_recv()
        rows_at = pl.ds(pl.multiple_of(group * 8, 8), 8)
        lanes_at = pl.ds(pl.multiple_of(pair * 2 * TILE, 2 * TILE), 2 * TILE)
        total = slot_ref[0, :, rows_at, lanes_at]
        for other in range(1, n_rep):
            total = total + slot_ref[other, :, rows_at, lanes_at]
        mean = total / n_rep
        velocity = friction * vel_ref[:, rows_at, lanes_at] + time_step * mean + noise_coef * noise_ref[:, rows_at, lanes_at]
        mean_ref[:, rows_at, lanes_at] = mean
        new_vel_ref[:, rows_at, lanes_at] = velocity
        new_pos_ref[:, rows_at, lanes_at] = pos_ref[:, rows_at, lanes_at] + time_step * velocity
        for hop in range(1, n_rep):
            rep_copy(hop, group, pair).wait_send()
        return carry

    lax.fori_loop(0, groups * pairs, finish, 0)
    for k, (dx, dy) in enumerate(directions):
        @pl.when(present(dx, dy))
        def _():
            halo_copy(k).wait_send()


def per_device(positions, velocities, noise, bonds):
    _, _, rows_local, lanes = positions.shape
    n_rep = lax.axis_size("rep")
    chunks = (rows_local // 8) * (lanes // (2 * TILE))
    wide = lanes + TILE
    plane = jax.ShapeDtypeStruct((3, rows_local, lanes), jnp.float32)
    vmem = pl.BlockSpec(memory_space=pltpu.VMEM)
    mean, velocity, position = pl.pallas_call(
        step_kernel,
        out_shape=[plane] * 3,
        in_specs=[vmem] * 4,
        out_specs=[vmem] * 3,
        scratch_shapes=[
            pltpu.VMEM((rows_local + 2, wide, TILE), jnp.bfloat16),
            pltpu.VMEM((rows_local + 2, 2, 16, wide), jnp.bfloat16),
            pltpu.VMEM((rows_local, 3, 64, lanes), jnp.bfloat16),
            pltpu.VMEM((rows_local, 8, lanes), jnp.float32),
            pltpu.VMEM((n_rep, 3, rows_local, lanes), jnp.float32),
            pltpu.VMEM((2, 8, lanes), jnp.float32),
            pltpu.VMEM((2, 8, lanes + 2 * TILE), jnp.float32),
            pltpu.VMEM((2, 3, rows_local, TILE), jnp.float32),
            pltpu.VMEM((8, 8, 2 * TILE), jnp.float32),
            pltpu.SemaphoreType.DMA((8,)),
            pltpu.SemaphoreType.DMA((8,)),
            pltpu.SemaphoreType.DMA((n_rep - 1, chunks)),
            pltpu.SemaphoreType.DMA((n_rep - 1, chunks)),
        ],
        compiler_params=pltpu.CompilerParams(
            vmem_limit_bytes=48 * 1024 * 1024, collective_id=0, has_side_effects=True
        ),
        name="forces_and_step",
    )(positions[0], velocities[0], noise[0], bond_bias(bonds))
    return mean, velocity[None], position[None]


def bond_bias(bonds):
    cols_local = bonds.shape[1]
    odd = (jnp.arange(cols_local) % 2 == 1)[None, :]
    rows = []
    for step in range(3):
        flags = [
            jnp.ones(bonds.shape[:2], bonds.dtype) if k < 0 else bonds[:, :, k] for k in offset_at[step]
        ]
        none = jnp.zeros_like(flags[0])
        for role in range(8):
            even_flag = flags[role] if role < 3 else none
            odd_flag = flags[role - 1] if 1 <= role < 4 else none
            rows.append(jnp.where(odd, odd_flag, even_flag))
    picked = jnp.stack(rows, axis=1)
    return jnp.where(picked != 0, 0.0, blocked).astype(jnp.float32)


def solution(mesh):
    in_specs = (
        P("rep", None, "gx", "gy"),
        P("rep", None, "gx", "gy"),
        P("rep", None, "gx", "gy"),
        P("gx", "gy", None),
    )
    out_specs = (P(None, "gx", "gy"), P("rep", None, "gx", "gy"), P("rep", None, "gx", "gy"))
    return jax.shard_map(
        per_device, mesh=mesh, in_specs=in_specs, out_specs=out_specs, check_vma=False
    )
```

```python
import jax
import jax.numpy as jnp
from jax import lax
from jax.experimental import pallas as pl
from jax.experimental.pallas import tpu as pltpu
from jax.sharding import PartitionSpec as P

ATOMS = 64
TILE = 128

spacing = 4.0
friction = 0.6
noise_coef = 0.8
time_step = 0.2
centre = 2.0
alpha = 0.5 * 1.4426950408889634
ratio = 4.0 ** (-1.0 / 3.0)
blocked = -16384.0
offset_at = ((7, 6, 5), (4, -1, 0), (1, 2, 3))


def iota(shape, axis):
    return lax.broadcasted_iota(jnp.int32, shape, axis)


def split3(value):
    first = value.astype(jnp.bfloat16).astype(jnp.float32)
    rest = value - first
    second = rest.astype(jnp.bfloat16).astype(jnp.float32)
    return first, second, rest - second


directions = ((-1, -1), (-1, 0), (-1, 1), (0, -1), (0, 1), (1, -1), (1, 0), (1, 1))
MESH = pl.DeviceIdType.MESH


def row_of(ref, row):
    sub = iota((8, ref.shape[2]), 0)
    pieces = [ref[d, pl.ds(row, 1), :] for d in range(3)]
    return jnp.where(sub == 0, pieces[0], jnp.where(sub == 1, pieces[1], jnp.where(sub == 2, pieces[2], 0.0)))


def bond_bias(bonds):
    cols = bonds.shape[0]
    flags = bonds.astype(jnp.float32).astype(jnp.bfloat16)
    place, offset = iota((24, 8), 0), iota((24, 8), 1)
    side = lax.rem(iota((24, cols), 1), 2)
    at = iota((24, cols), 0)
    picked = []
    for odd in range(2):
        pick = jnp.zeros((24, 8), jnp.float32)
        for step in range(3):
            for role in range(3):
                if offset_at[step][role] >= 0:
                    here = (place == 8 * step + role + odd) & (offset == offset_at[step][role])
                    pick = jnp.where(here, 1.0, pick)
        picked.append(
            lax.dot_general(
                pick.astype(jnp.bfloat16), flags, (((1,), (1,)), ((), ())), preferred_element_type=jnp.float32
            )
        )
    flag = jnp.where(side == 0, picked[0], picked[1])
    flag = jnp.where(at == 9 + side, 1.0, flag)
    return ((1.0 - flag) * blocked).astype(jnp.bfloat16)


def step_kernel(
    pos_ref, vel_ref, noise_ref, bond_ref,
    mean_ref, new_vel_ref, new_pos_ref,
    lhs_ref, coef_ref, common_ref, rhs_ref, base_ref, slot_ref, stage_ref, row_ref, col_ref, hold_ref,
    halo_send, halo_recv, rep_send, rep_recv,
):
    _, rows_local, lanes = pos_ref.shape
    cols_local = lanes // ATOMS
    tiles = lanes // TILE
    wide = lanes + TILE
    pairs = tiles // 2
    groups = rows_local // 8
    gx, gy, rep = lax.axis_index("gx"), lax.axis_index("gy"), lax.axis_index("rep")
    n_gx, n_gy, n_rep = lax.axis_size("gx"), lax.axis_size("gy"), lax.axis_size("rep")

    def present(dx, dy):
        checks = []
        if dx < 0:
            checks.append(gx > 0)
        if dx > 0:
            checks.append(gx < n_gx - 1)
        if dy < 0:
            checks.append(gy > 0)
        if dy > 0:
            checks.append(gy < n_gy - 1)
        found = checks[0]
        for check in checks[1:]:
            found = found & check
        return found

    barrier = pltpu.get_barrier_semaphore()
    expected = jnp.int32(n_rep - 1)
    for dx, dy in directions:
        there = present(dx, dy)
        expected = expected + there.astype(jnp.int32)

        @pl.when(there)
        def _():
            pl.semaphore_signal(barrier, inc=1, device_id={"gx": gx + dx, "gy": gy + dy}, device_id_type=MESH)

    for hop in range(1, n_rep):
        pl.semaphore_signal(barrier, inc=1, device_id={"rep": lax.rem(rep + hop, n_rep)}, device_id_type=MESH)

    stage_ref[0] = row_of(pos_ref, 0)
    stage_ref[1] = row_of(pos_ref, rows_local - 1)

    def halo_place(dx, dy):
        side = 0 if dx > 0 else 1
        if dx == 0:
            source = pos_ref.at[:, :, pl.ds(lanes - TILE if dy > 0 else 0, TILE)]
            return source, col_ref.at[0 if dy > 0 else 1]
        if dy == 0:
            return stage_ref.at[1 if dx > 0 else 0], row_ref.at[side, :, pl.ds(TILE, lanes)]
        source = stage_ref.at[1 if dx > 0 else 0, :, pl.ds(lanes - TILE if dy > 0 else 0, TILE)]
        return source, row_ref.at[side, :, pl.ds(0 if dy > 0 else TILE + lanes, TILE)]

    def halo_copy(k):
        dx, dy = directions[k]
        source, target = halo_place(dx, dy)
        return pltpu.make_async_remote_copy(
            src_ref=source, dst_ref=target, send_sem=halo_send.at[k], recv_sem=halo_recv.at[k],
            device_id={"gx": gx + dx, "gy": gy + dy}, device_id_type=MESH,
        )

    pl.semaphore_wait(barrier, expected)
    for k, (dx, dy) in enumerate(directions):
        @pl.when(present(dx, dy))
        def _():
            halo_copy(k).start()

    def own_row(row, carry):
        sub = iota((8, lanes), 0)
        half = lax.rem(iota((8, lanes), 1) // ATOMS, 2).astype(jnp.float32)
        expand = (iota((cols_local, lanes), 1) // ATOMS == iota((cols_local, lanes), 0)).astype(jnp.bfloat16)
        bias = jnp.dot(bond_bias(bond_ref[row]), expand, preferred_element_type=jnp.float32)
        base = row_of(pos_ref, row) - centre
        base = base + jnp.where(sub == 1, (half - 0.5) * spacing, 0.0)
        base = jnp.where(sub < 3, base, 0.0)
        base_ref[row] = base
        square = 2.0 / 3.0 - alpha * jnp.sum(base * base, axis=0, keepdims=True)
        one, two, three = split3(jnp.where(sub == 3, 1.0, jnp.where(sub == 4, square, base)))
        common_ref[row] = jnp.concatenate([one, two, three, one, two, one], axis=0).astype(jnp.bfloat16)
        for step in range(3):
            dx = step - 1
            extra = jnp.zeros((8, lanes), jnp.float32)
            if dx != 0:
                shift = jnp.broadcast_to(alpha * (2.0 * dx * spacing * base[0:1] - spacing * spacing), (8, lanes))
                one, two, three = split3(shift)
                extra = jnp.where(sub == 3, one, jnp.where(sub == 4, two, jnp.where(sub == 5, three, extra)))
                extra = jnp.where(sub < 3, -spacing * dx, extra)
            rhs_ref[row, step] = jnp.concatenate([bias[8 * step : 8 * step + 8], extra], axis=0).astype(jnp.bfloat16)
        return carry

    lax.fori_loop(0, rows_local, own_row, 0)

    for k, (dx, dy) in enumerate(directions):
        @pl.when(present(-dx, -dy))
        def _():
            halo_copy(k).wait_recv()

        @pl.when(jnp.logical_not(present(-dx, -dy)))
        def _():
            target = halo_place(dx, dy)[1]
            target[...] = jnp.zeros(target.shape, jnp.float32)

    def features(row, whole_row):
        sub = iota((8, wide), 0)
        slot = iota((8, wide), 1) // ATOMS
        base = pltpu.roll(whole_row, wide + TILE - ATOMS, 1)[:, :wide] - centre
        stacked = []
        for parity in range(2):
            role = lax.rem(slot + 2 * parity, 4)
            moved = base + jnp.where(sub == 1, (role.astype(jnp.float32) - 1.5) * spacing, 0.0)
            moved = jnp.where(sub < 3, moved, 0.0)
            square = -alpha * jnp.sum(moved * moved, axis=0, keepdims=True)
            vec = jnp.where(sub == 3, square, jnp.where(sub == 4, 1.0, 2.0 * alpha * moved))
            one, two, three = split3(vec)
            hot = jnp.where(sub == role, 1.0, 0.0)
            along = jnp.where(sub == 0, one[0:1], jnp.where(sub == 1, two[0:1], three[0:1]))
            along = jnp.where(sub < 3, along, jnp.where(sub < 6, 1.0, 0.0))
            stacked += [one, one, one, two, two, three, hot, along]
            coef_ref[row, parity] = jnp.concatenate([one, two], axis=0).astype(jnp.bfloat16)
        whole = jnp.concatenate(stacked, axis=0).astype(jnp.bfloat16)
        for t in range(wide // TILE):
            lhs_ref[row, t * TILE : (t + 1) * TILE] = whole[:, t * TILE : (t + 1) * TILE].T

    def inner_features(row, carry):
        features(row + 1, jnp.concatenate([row_of(col_ref.at[0], row), row_of(pos_ref, row), row_of(col_ref.at[1], row)], axis=1))
        return carry

    lax.fori_loop(0, rows_local, inner_features, 0)
    features(0, row_ref[0])
    features(rows_local + 1, row_ref[1])

    def weights(lhs, rhs):
        soft = jnp.exp2(jnp.dot(lhs, rhs, preferred_element_type=jnp.float32))
        square = soft * soft
        weight = square * square - soft
        high = weight.astype(jnp.bfloat16)
        return high, (weight - high.astype(jnp.float32)).astype(jnp.bfloat16)

    def rep_copy(hop, group, pair):
        chunk = slot_ref.at[
            rep, :, pl.ds(pl.multiple_of(group * 8, 8), 8), pl.ds(pl.multiple_of(pair * 2 * TILE, 2 * TILE), 2 * TILE)
        ]
        return pltpu.make_async_remote_copy(
            src_ref=chunk, dst_ref=chunk,
            send_sem=rep_send.at[hop - 1, group * pairs + pair], recv_sem=rep_recv.at[hop - 1, group * pairs + pair],
            device_id={"rep": lax.rem(rep + hop, n_rep)}, device_id_type=MESH,
        )

    def tile_rows(row, place, start, parity):
        lanes_at = pl.ds(start, TILE)
        shifts = [jnp.where(iota((8, TILE), 0) == 0, (step - 1) * spacing, 0.0) for step in range(3)]
        bases = [base_ref[row + r, :, lanes_at] for r in range(2)]
        totals = [jnp.zeros((8, TILE), jnp.float32) for _ in range(2)]

        def feat(r, step):
            block = jnp.concatenate([common_ref[row + r, :, lanes_at], rhs_ref[row + r, step, :, lanes_at]], axis=0)
            none = jnp.zeros_like(block)
            return jnp.concatenate([block, none] if parity == 0 else [none, block], axis=0)

        for q in range(4):
            lhs = lhs_ref[row + q, pl.ds(start, 2 * TILE)]
            coef = coef_ref[row + q, parity, :, pl.ds(start, 2 * TILE)]
            served = [(r, q - r) for r in range(2) if 0 <= q - r < 3]
            rhs = jnp.concatenate([feat(r, step) for r, step in served], axis=1)
            high, low = weights(lhs, rhs)
            if len(served) == 1:
                sums = jnp.dot(coef, jnp.concatenate([high, low], axis=1), preferred_element_type=jnp.float32)
                sums = sums[:, :TILE] + sums[:, TILE:]
            else:
                sums = jnp.dot(coef, high, preferred_element_type=jnp.float32)
                sums = sums + jnp.dot(coef, low, preferred_element_type=jnp.float32)
            sums = sums[0:8] + sums[8:16]
            for at, (r, step) in enumerate(served):
                part = sums[:, at * TILE : (at + 1) * TILE]
                totals[r] = totals[r] + (bases[r] - shifts[step]) * part[4:5] - (0.5 / alpha) * part
        for r in range(2):
            hold_ref[place + r, :, parity * TILE : (parity + 1) * TILE] = (0.5 * ratio) * totals[r]

    def chunk_step(at, carry):
        group, pair = at // pairs, lax.rem(at, pairs)

        def row_pair(inner, unused):
            for parity in range(2):
                start = pl.multiple_of((2 * pair + parity) * TILE, TILE)
                tile_rows(group * 8 + inner * 2, inner * 2, start, parity)
            return unused

        lax.fori_loop(0, 4, row_pair, 0)
        sub = iota((8, 2 * TILE), 0)
        for d in range(3):
            block = jnp.zeros((8, 2 * TILE), jnp.float32)
            for r in range(8):
                block = jnp.where(sub == r, hold_ref[r, d : d + 1], block)
            slot_ref[
                rep, d, pl.ds(pl.multiple_of(group * 8, 8), 8), pl.ds(pl.multiple_of(pair * 2 * TILE, 2 * TILE), 2 * TILE)
            ] = block
        for hop in range(1, n_rep):
            rep_copy(hop, group, pair).start()
        return carry

    lax.fori_loop(0, groups * pairs, chunk_step, 0)

    def finish(at, carry):
        group, pair = at // pairs, lax.rem(at, pairs)
        for hop in range(1, n_rep):
            chunk = slot_ref.at[
                lax.rem(rep + n_rep - hop, n_rep), :,
                pl.ds(pl.multiple_of(group * 8, 8), 8), pl.ds(pl.multiple_of(pair * 2 * TILE, 2 * TILE), 2 * TILE),
            ]
            pltpu.make_async_remote_copy(
                src_ref=chunk, dst_ref=chunk,
                send_sem=rep_send.at[hop - 1, at], recv_sem=rep_recv.at[hop - 1, at],
                device_id={"rep": lax.rem(rep + hop, n_rep)}, device_id_type=MESH,
            ).wait_recv()
        rows_at = pl.ds(pl.multiple_of(group * 8, 8), 8)
        lanes_at = pl.ds(pl.multiple_of(pair * 2 * TILE, 2 * TILE), 2 * TILE)
        total = slot_ref[0, :, rows_at, lanes_at]
        for other in range(1, n_rep):
            total = total + slot_ref[other, :, rows_at, lanes_at]
        mean = total / n_rep
        velocity = friction * vel_ref[:, rows_at, lanes_at] + time_step * mean + noise_coef * noise_ref[:, rows_at, lanes_at]
        mean_ref[:, rows_at, lanes_at] = mean
        new_vel_ref[:, rows_at, lanes_at] = velocity
        new_pos_ref[:, rows_at, lanes_at] = pos_ref[:, rows_at, lanes_at] + time_step * velocity
        for hop in range(1, n_rep):
            rep_copy(hop, group, pair).wait_send()
        return carry

    lax.fori_loop(0, groups * pairs, finish, 0)
    for k, (dx, dy) in enumerate(directions):
        @pl.when(present(dx, dy))
        def _():
            halo_copy(k).wait_send()


def per_device(positions, velocities, noise, bonds):
    _, _, rows_local, lanes = positions.shape
    n_rep = lax.axis_size("rep")
    chunks = (rows_local // 8) * (lanes // (2 * TILE))
    wide = lanes + TILE
    plane = jax.ShapeDtypeStruct((3, rows_local, lanes), jnp.float32)
    vmem = pl.BlockSpec(memory_space=pltpu.VMEM)
    mean, velocity, position = pl.pallas_call(
        step_kernel,
        out_shape=[plane] * 3,
        in_specs=[vmem] * 4,
        out_specs=[vmem] * 3,
        scratch_shapes=[
            pltpu.VMEM((rows_local + 2, wide, TILE), jnp.bfloat16),
            pltpu.VMEM((rows_local + 2, 2, 16, wide), jnp.bfloat16),
            pltpu.VMEM((rows_local, 48, lanes), jnp.bfloat16),
            pltpu.VMEM((rows_local, 3, 16, lanes), jnp.bfloat16),
            pltpu.VMEM((rows_local, 8, lanes), jnp.float32),
            pltpu.VMEM((n_rep, 3, rows_local, lanes), jnp.float32),
            pltpu.VMEM((2, 8, lanes), jnp.float32),
            pltpu.VMEM((2, 8, lanes + 2 * TILE), jnp.float32),
            pltpu.VMEM((2, 3, rows_local, TILE), jnp.float32),
            pltpu.VMEM((8, 8, 2 * TILE), jnp.float32),
            pltpu.SemaphoreType.DMA((8,)),
            pltpu.SemaphoreType.DMA((8,)),
            pltpu.SemaphoreType.DMA((n_rep - 1, chunks)),
            pltpu.SemaphoreType.DMA((n_rep - 1, chunks)),
        ],
        compiler_params=pltpu.CompilerParams(
            vmem_limit_bytes=48 * 1024 * 1024, collective_id=0, has_side_effects=True
        ),
        name="forces_and_step",
    )(positions[0], velocities[0], noise[0], bonds)
    return mean, velocity[None], position[None]


def solution(mesh):
    in_specs = (
        P("rep", None, "gx", "gy"),
        P("rep", None, "gx", "gy"),
        P("rep", None, "gx", "gy"),
        P("gx", "gy", None),
    )
    out_specs = (P(None, "gx", "gy"), P("rep", None, "gx", "gy"), P("rep", None, "gx", "gy"))
    return jax.shard_map(
        per_device, mesh=mesh, in_specs=in_specs, out_specs=out_specs, check_vma=False
    )
```

```python
import jax
import jax.numpy as jnp
from jax import lax
from jax.experimental import pallas as pl
from jax.experimental.pallas import tpu as pltpu
from jax.sharding import PartitionSpec as P

ATOMS = 64
TILE = 128

spacing = 4.0
friction = 0.6
noise_coef = 0.8
time_step = 0.2
centre = 2.0
alpha = 0.5 * 1.4426950408889634
ratio = 4.0 ** (-1.0 / 3.0)
blocked = -16384.0
offset_at = ((7, 6, 5), (4, -1, 0), (1, 2, 3))


def iota(shape, axis):
    return lax.broadcasted_iota(jnp.int32, shape, axis)


def split3(value):
    first = value.astype(jnp.bfloat16).astype(jnp.float32)
    rest = value - first
    second = rest.astype(jnp.bfloat16).astype(jnp.float32)
    return first, second, rest - second


directions = ((-1, -1), (-1, 0), (-1, 1), (0, -1), (0, 1), (1, -1), (1, 0), (1, 1))
MESH = pl.DeviceIdType.MESH


def row_of(ref, row):
    sub = iota((8, ref.shape[2]), 0)
    pieces = [ref[d, pl.ds(row, 1), :] for d in range(3)]
    return jnp.where(sub == 0, pieces[0], jnp.where(sub == 1, pieces[1], jnp.where(sub == 2, pieces[2], 0.0)))


def bond_bias(bonds):
    cols = bonds.shape[0]
    flags = bonds.astype(jnp.float32).astype(jnp.bfloat16)
    place, offset = iota((24, 8), 0), iota((24, 8), 1)
    side = lax.rem(iota((24, cols), 1), 2)
    at = iota((24, cols), 0)
    picked = []
    for odd in range(2):
        pick = jnp.zeros((24, 8), jnp.float32)
        for step in range(3):
            for role in range(3):
                if offset_at[step][role] >= 0:
                    here = (place == 8 * step + role + odd) & (offset == offset_at[step][role])
                    pick = jnp.where(here, 1.0, pick)
        picked.append(
            lax.dot_general(
                pick.astype(jnp.bfloat16), flags, (((1,), (1,)), ((), ())), preferred_element_type=jnp.float32
            )
        )
    flag = jnp.where(side == 0, picked[0], picked[1])
    flag = jnp.where(at == 9 + side, 1.0, flag)
    return ((1.0 - flag) * blocked).astype(jnp.bfloat16)


def step_kernel(
    pos_ref, vel_far, noise_far, bond_ref,
    mean_ref, new_vel_ref, new_pos_ref,
    lhs_ref, coef_ref, common_ref, rhs_ref, base_ref, slot_ref, stage_ref, row_ref, col_ref, hold_ref,
    vel_ref, noise_ref, load_sem, halo_send, halo_recv, rep_send, rep_recv,
):
    _, rows_local, lanes = pos_ref.shape
    cols_local = lanes // ATOMS
    tiles = lanes // TILE
    wide = lanes + TILE
    pairs = tiles // 2
    groups = rows_local // 8
    gx, gy, rep = lax.axis_index("gx"), lax.axis_index("gy"), lax.axis_index("rep")
    n_gx, n_gy, n_rep = lax.axis_size("gx"), lax.axis_size("gy"), lax.axis_size("rep")

    def present(dx, dy):
        checks = []
        if dx < 0:
            checks.append(gx > 0)
        if dx > 0:
            checks.append(gx < n_gx - 1)
        if dy < 0:
            checks.append(gy > 0)
        if dy > 0:
            checks.append(gy < n_gy - 1)
        found = checks[0]
        for check in checks[1:]:
            found = found & check
        return found

    loads = [
        pltpu.make_async_copy(vel_far, vel_ref, load_sem.at[0]),
        pltpu.make_async_copy(noise_far, noise_ref, load_sem.at[1]),
    ]
    for load in loads:
        load.start()
    barrier = pltpu.get_barrier_semaphore()
    expected = jnp.int32(n_rep - 1)
    for dx, dy in directions:
        there = present(dx, dy)
        expected = expected + there.astype(jnp.int32)

        @pl.when(there)
        def _():
            pl.semaphore_signal(barrier, inc=1, device_id={"gx": gx + dx, "gy": gy + dy}, device_id_type=MESH)

    for hop in range(1, n_rep):
        pl.semaphore_signal(barrier, inc=1, device_id={"rep": lax.rem(rep + hop, n_rep)}, device_id_type=MESH)

    stage_ref[0] = row_of(pos_ref, 0)
    stage_ref[1] = row_of(pos_ref, rows_local - 1)

    def halo_place(dx, dy):
        side = 0 if dx > 0 else 1
        if dx == 0:
            source = pos_ref.at[:, :, pl.ds(lanes - TILE if dy > 0 else 0, TILE)]
            return source, col_ref.at[0 if dy > 0 else 1]
        if dy == 0:
            return stage_ref.at[1 if dx > 0 else 0], row_ref.at[side, :, pl.ds(TILE, lanes)]
        source = stage_ref.at[1 if dx > 0 else 0, :, pl.ds(lanes - TILE if dy > 0 else 0, TILE)]
        return source, row_ref.at[side, :, pl.ds(0 if dy > 0 else TILE + lanes, TILE)]

    def halo_copy(k):
        dx, dy = directions[k]
        source, target = halo_place(dx, dy)
        return pltpu.make_async_remote_copy(
            src_ref=source, dst_ref=target, send_sem=halo_send.at[k], recv_sem=halo_recv.at[k],
            device_id={"gx": gx + dx, "gy": gy + dy}, device_id_type=MESH,
        )

    pl.semaphore_wait(barrier, expected)
    for k, (dx, dy) in enumerate(directions):
        @pl.when(present(dx, dy))
        def _():
            halo_copy(k).start()

    def own_row(row, carry):
        sub = iota((8, lanes), 0)
        half = lax.rem(iota((8, lanes), 1) // ATOMS, 2).astype(jnp.float32)
        expand = (iota((cols_local, lanes), 1) // ATOMS == iota((cols_local, lanes), 0)).astype(jnp.bfloat16)
        bias = jnp.dot(bond_bias(bond_ref[row]), expand, preferred_element_type=jnp.float32)
        base = row_of(pos_ref, row) - centre
        base = base + jnp.where(sub == 1, (half - 0.5) * spacing, 0.0)
        base = jnp.where(sub < 3, base, 0.0)
        base_ref[row] = base
        square = 2.0 / 3.0 - alpha * jnp.sum(base * base, axis=0, keepdims=True)
        one, two, three = split3(jnp.where(sub == 3, 1.0, jnp.where(sub == 4, square, base)))
        common = jnp.concatenate([one, two, three, one, two, one], axis=0)
        left = half[0:1] == 0.0
        common_ref[row, 0] = common.astype(jnp.bfloat16)
        common_ref[row, 1] = jnp.where(left, common, 0.0).astype(jnp.bfloat16)
        common_ref[row, 2] = jnp.where(left, 0.0, common).astype(jnp.bfloat16)
        for step in range(3):
            dx = step - 1
            extra = jnp.zeros((8, lanes), jnp.float32)
            if dx != 0:
                shift = jnp.broadcast_to(alpha * (2.0 * dx * spacing * base[0:1] - spacing * spacing), (8, lanes))
                one, two, three = split3(shift)
                extra = jnp.where(sub == 3, one, jnp.where(sub == 4, two, jnp.where(sub == 5, three, extra)))
                extra = jnp.where(sub < 3, -spacing * dx, extra)
            other = jnp.concatenate([bias[8 * step : 8 * step + 8], extra], axis=0)
            rhs_ref[row, step, 0] = other.astype(jnp.bfloat16)
            rhs_ref[row, step, 1] = jnp.where(left, other, 0.0).astype(jnp.bfloat16)
            rhs_ref[row, step, 2] = jnp.where(left, 0.0, other).astype(jnp.bfloat16)
        return carry

    lax.fori_loop(0, rows_local, own_row, 0)

    for k, (dx, dy) in enumerate(directions):
        @pl.when(present(-dx, -dy))
        def _():
            halo_copy(k).wait_recv()

        @pl.when(jnp.logical_not(present(-dx, -dy)))
        def _():
            target = halo_place(dx, dy)[1]
            target[...] = jnp.zeros(target.shape, jnp.float32)

    def features(row, whole_row):
        sub = iota((8, wide), 0)
        slot = iota((8, wide), 1) // ATOMS
        base = pltpu.roll(whole_row, wide + TILE - ATOMS, 1)[:, :wide] - centre
        stacked, splits = [], []
        for kind in range(2):
            role = lax.rem(slot, 2) + 2 * kind
            moved = base + jnp.where(sub == 1, (role.astype(jnp.float32) - 1.5) * spacing, 0.0)
            moved = jnp.where(sub < 3, moved, 0.0)
            square = -alpha * jnp.sum(moved * moved, axis=0, keepdims=True)
            vec = jnp.where(sub == 3, square, jnp.where(sub == 4, 1.0, 2.0 * alpha * moved))
            one, two, three = split3(vec)
            hot = jnp.where(sub == role, 1.0, 0.0)
            along = jnp.where(sub == 0, one[0:1], jnp.where(sub == 1, two[0:1], three[0:1]))
            along = jnp.where(sub < 3, along, jnp.where(sub < 6, 1.0, 0.0))
            stacked += [one, one, one, two, two, three, hot, along]
            splits.append(jnp.concatenate([one, two], axis=0))
        far = pltpu.roll(splits[1], wide - TILE - ATOMS, 1)
        mixed = jnp.where(lax.rem(iota((16, wide), 1), TILE) < ATOMS, far, splits[0])
        coef_ref[row, 0] = jnp.concatenate([splits[0], mixed], axis=0).astype(jnp.bfloat16)
        coef_ref[row, 1] = jnp.concatenate([splits[1], splits[1]], axis=0).astype(jnp.bfloat16)
        whole = jnp.concatenate(stacked, axis=0)
        left = iota((ATOMS, TILE), 1) < ATOMS
        before = None
        for t in range(wide // TILE):
            turned = whole[:, t * TILE : (t + 1) * TILE].T
            even, odd = turned[:ATOMS], turned[ATOMS:]
            if t > 0:
                lhs_ref[row, t - 1, 0:ATOMS] = jnp.where(left, before, odd).astype(jnp.bfloat16)
                lhs_ref[row, t - 1, 2 * ATOMS : 3 * ATOMS] = jnp.where(left, 0.0, even).astype(jnp.bfloat16)
            if t < tiles:
                lhs_ref[row, t, ATOMS : 2 * ATOMS] = jnp.where(left, odd, 0.0).astype(jnp.bfloat16)
            before = even

    def inner_features(row, carry):
        features(row + 1, jnp.concatenate([row_of(col_ref.at[0], row), row_of(pos_ref, row), row_of(col_ref.at[1], row)], axis=1))
        return carry

    lax.fori_loop(0, rows_local, inner_features, 0)
    features(0, row_ref[0])
    features(rows_local + 1, row_ref[1])

    def weights(lhs, outer, full):
        power = jnp.concatenate(
            [
                jnp.dot(lhs[:ATOMS], outer, preferred_element_type=jnp.float32),
                jnp.dot(lhs[ATOMS:], full, preferred_element_type=jnp.float32),
            ],
            axis=0,
        )
        soft = jnp.exp2(power)
        square = soft * soft
        weight = square * square - soft
        high = weight.astype(jnp.bfloat16)
        return high, (weight - high.astype(jnp.float32)).astype(jnp.bfloat16)

    def rep_copy(hop, group, pair):
        chunk = slot_ref.at[
            rep, :, pl.ds(pl.multiple_of(group * 8, 8), 8), pl.ds(pl.multiple_of(pair * 2 * TILE, 2 * TILE), 2 * TILE)
        ]
        return pltpu.make_async_remote_copy(
            src_ref=chunk, dst_ref=chunk,
            send_sem=rep_send.at[hop - 1, group * pairs + pair], recv_sem=rep_recv.at[hop - 1, group * pairs + pair],
            device_id={"rep": lax.rem(rep + hop, n_rep)}, device_id_type=MESH,
        )

    def tile_rows(row, place, tile, start, parity):
        lanes_at = pl.ds(start, TILE)
        shifts = [jnp.where(iota((8, TILE), 0) == 0, (step - 1) * spacing, 0.0) for step in range(3)]
        bases = [base_ref[row + r, :, lanes_at] for r in range(2)]
        totals = [jnp.zeros((8, TILE), jnp.float32) for _ in range(2)]

        def feat(r, step, part):
            return jnp.concatenate(
                [common_ref[row + r, part, :, lanes_at], rhs_ref[row + r, step, part, :, lanes_at]], axis=0
            )

        left = iota((16, TILE), 1) < ATOMS
        for q in range(4):
            lhs = lhs_ref[row + q, tile]
            coef = jnp.concatenate(
                [coef_ref[row + q, 0, :, lanes_at], coef_ref[row + q, 1, :, pl.ds(start + TILE, TILE)]], axis=1
            )[:, : 3 * ATOMS]
            served = [(r, q - r) for r in range(2) if 0 <= q - r < 3]
            outer = jnp.concatenate(
                [jnp.concatenate([feat(r, step, 1), feat(r, step, 2)], axis=0) for r, step in served], axis=1
            )
            full = jnp.concatenate([feat(r, step, 0) for r, step in served], axis=1)
            high, low = weights(lhs, outer, jnp.concatenate([full, full], axis=0))
            if len(served) == 1:
                sums = jnp.dot(coef, jnp.concatenate([high, low], axis=1), preferred_element_type=jnp.float32)
                sums = sums[:, :TILE] + sums[:, TILE:]
            else:
                sums = jnp.dot(coef, high, preferred_element_type=jnp.float32)
                sums = sums + jnp.dot(coef, low, preferred_element_type=jnp.float32)
            for at, (r, step) in enumerate(served):
                part = sums[:, at * TILE : (at + 1) * TILE]
                part = jnp.where(left, part[0:16], part[16:32])
                part = part[0:8] + part[8:16]
                totals[r] = totals[r] + (bases[r] - shifts[step]) * part[4:5] - (0.5 / alpha) * part
        for r in range(2):
            hold_ref[place + r, :, parity * TILE : (parity + 1) * TILE] = (0.5 * ratio) * totals[r]

    def chunk_step(at, carry):
        group, pair = at // pairs, lax.rem(at, pairs)

        def row_pair(inner, unused):
            for parity in range(2):
                start = pl.multiple_of((2 * pair + parity) * TILE, TILE)
                tile_rows(group * 8 + inner * 2, inner * 2, 2 * pair + parity, start, parity)
            return unused

        lax.fori_loop(0, 4, row_pair, 0)
        sub = iota((8, 2 * TILE), 0)
        for d in range(3):
            block = jnp.zeros((8, 2 * TILE), jnp.float32)
            for r in range(8):
                block = jnp.where(sub == r, hold_ref[r, d : d + 1], block)
            slot_ref[
                rep, d, pl.ds(pl.multiple_of(group * 8, 8), 8), pl.ds(pl.multiple_of(pair * 2 * TILE, 2 * TILE), 2 * TILE)
            ] = block
        for hop in range(1, n_rep):
            rep_copy(hop, group, pair).start()
        return carry

    lax.fori_loop(0, groups * pairs, chunk_step, 0)

    for load in loads:
        load.wait()

    def finish(at, carry):
        group, pair = at // pairs, lax.rem(at, pairs)
        for hop in range(1, n_rep):
            chunk = slot_ref.at[
                lax.rem(rep + n_rep - hop, n_rep), :,
                pl.ds(pl.multiple_of(group * 8, 8), 8), pl.ds(pl.multiple_of(pair * 2 * TILE, 2 * TILE), 2 * TILE),
            ]
            pltpu.make_async_remote_copy(
                src_ref=chunk, dst_ref=chunk,
                send_sem=rep_send.at[hop - 1, at], recv_sem=rep_recv.at[hop - 1, at],
                device_id={"rep": lax.rem(rep + hop, n_rep)}, device_id_type=MESH,
            ).wait_recv()
        rows_at = pl.ds(pl.multiple_of(group * 8, 8), 8)
        lanes_at = pl.ds(pl.multiple_of(pair * 2 * TILE, 2 * TILE), 2 * TILE)
        total = slot_ref[0, :, rows_at, lanes_at]
        for other in range(1, n_rep):
            total = total + slot_ref[other, :, rows_at, lanes_at]
        mean = total / n_rep
        velocity = friction * vel_ref[:, rows_at, lanes_at] + time_step * mean + noise_coef * noise_ref[:, rows_at, lanes_at]
        mean_ref[:, rows_at, lanes_at] = mean
        new_vel_ref[:, rows_at, lanes_at] = velocity
        new_pos_ref[:, rows_at, lanes_at] = pos_ref[:, rows_at, lanes_at] + time_step * velocity
        for hop in range(1, n_rep):
            rep_copy(hop, group, pair).wait_send()
        return carry

    lax.fori_loop(0, groups * pairs, finish, 0)
    for k, (dx, dy) in enumerate(directions):
        @pl.when(present(dx, dy))
        def _():
            halo_copy(k).wait_send()


def per_device(positions, velocities, noise, bonds):
    _, _, rows_local, lanes = positions.shape
    n_rep = lax.axis_size("rep")
    chunks = (rows_local // 8) * (lanes // (2 * TILE))
    wide = lanes + TILE
    plane = jax.ShapeDtypeStruct((3, rows_local, lanes), jnp.float32)
    vmem = pl.BlockSpec(memory_space=pltpu.VMEM)
    mean, velocity, position = pl.pallas_call(
        step_kernel,
        out_shape=[plane] * 3,
        in_specs=[vmem, pl.BlockSpec(memory_space=pl.ANY), pl.BlockSpec(memory_space=pl.ANY), vmem],
        out_specs=[vmem] * 3,
        scratch_shapes=[
            pltpu.VMEM((rows_local + 2, lanes // TILE, 3 * ATOMS, TILE), jnp.bfloat16),
            pltpu.VMEM((rows_local + 2, 2, 32, wide), jnp.bfloat16),
            pltpu.VMEM((rows_local, 3, 48, lanes), jnp.bfloat16),
            pltpu.VMEM((rows_local, 3, 3, 16, lanes), jnp.bfloat16),
            pltpu.VMEM((rows_local, 8, lanes), jnp.float32),
            pltpu.VMEM((n_rep, 3, rows_local, lanes), jnp.float32),
            pltpu.VMEM((2, 8, lanes), jnp.float32),
            pltpu.VMEM((2, 8, lanes + 2 * TILE), jnp.float32),
            pltpu.VMEM((2, 3, rows_local, TILE), jnp.float32),
            pltpu.VMEM((8, 8, 2 * TILE), jnp.float32),
            pltpu.VMEM((3, rows_local, lanes), jnp.float32),
            pltpu.VMEM((3, rows_local, lanes), jnp.float32),
            pltpu.SemaphoreType.DMA((2,)),
            pltpu.SemaphoreType.DMA((8,)),
            pltpu.SemaphoreType.DMA((8,)),
            pltpu.SemaphoreType.DMA((n_rep - 1, chunks)),
            pltpu.SemaphoreType.DMA((n_rep - 1, chunks)),
        ],
        compiler_params=pltpu.CompilerParams(
            vmem_limit_bytes=58 * 1024 * 1024, collective_id=0, has_side_effects=True
        ),
        name="forces_and_step",
    )(positions[0], velocities[0], noise[0], bonds)
    return mean, velocity[None], position[None]


def solution(mesh):
    in_specs = (
        P("rep", None, "gx", "gy"),
        P("rep", None, "gx", "gy"),
        P("rep", None, "gx", "gy"),
        P("gx", "gy", None),
    )
    out_specs = (P(None, "gx", "gy"), P("rep", None, "gx", "gy"), P("rep", None, "gx", "gy"))
    return jax.shard_map(
        per_device, mesh=mesh, in_specs=in_specs, out_specs=out_specs, check_vma=False
    )
```

```python
import jax
import jax.numpy as jnp
from jax import lax
from jax.experimental import pallas as pl
from jax.experimental.pallas import tpu as pltpu
from jax.sharding import PartitionSpec as P

ATOMS = 64
TILE = 128

spacing = 4.0
friction = 0.6
noise_coef = 0.8
time_step = 0.2
centre = 2.0
alpha = 0.5 * 1.4426950408889634
ratio = 4.0 ** (-1.0 / 3.0)
blocked = -16384.0
offset_at = ((7, 6, 5), (4, -1, 0), (1, 2, 3))


def iota(shape, axis):
    return lax.broadcasted_iota(jnp.int32, shape, axis)


def split3(value):
    first = value.astype(jnp.bfloat16).astype(jnp.float32)
    rest = value - first
    second = rest.astype(jnp.bfloat16).astype(jnp.float32)
    return first, second, rest - second


directions = ((-1, -1), (-1, 0), (-1, 1), (0, -1), (0, 1), (1, -1), (1, 0), (1, 1))
MESH = pl.DeviceIdType.MESH


def row_of(ref, row):
    sub = iota((8, ref.shape[2]), 0)
    pieces = [ref[d, pl.ds(row, 1), :] for d in range(3)]
    return jnp.where(sub == 0, pieces[0], jnp.where(sub == 1, pieces[1], jnp.where(sub == 2, pieces[2], 0.0)))


def bond_bias(bonds):
    cols = bonds.shape[0]
    flags = bonds.astype(jnp.float32).astype(jnp.bfloat16)
    place, offset = iota((24, 8), 0), iota((24, 8), 1)
    side = lax.rem(iota((24, cols), 1), 2)
    at = iota((24, cols), 0)
    picked = []
    for odd in range(2):
        pick = jnp.zeros((24, 8), jnp.float32)
        for step in range(3):
            for role in range(3):
                if offset_at[step][role] >= 0:
                    here = (place == 8 * step + role + odd) & (offset == offset_at[step][role])
                    pick = jnp.where(here, 1.0, pick)
        picked.append(
            lax.dot_general(
                pick.astype(jnp.bfloat16), flags, (((1,), (1,)), ((), ())), preferred_element_type=jnp.float32
            )
        )
    flag = jnp.where(side == 0, picked[0], picked[1])
    flag = jnp.where(at == 9 + side, 1.0, flag)
    return ((1.0 - flag) * blocked).astype(jnp.bfloat16)


def step_kernel(
    pos_ref, vel_far, noise_far, bond_ref,
    mean_ref, new_vel_ref, new_pos_ref,
    lhs_ref, coef_ref, common_ref, rhs_ref, base_ref, slot_ref, stage_ref, row_ref, col_ref, hold_ref,
    vel_ref, noise_ref, load_sem, halo_send, halo_recv, rep_send, rep_recv,
):
    _, rows_local, lanes = pos_ref.shape
    cols_local = lanes // ATOMS
    tiles = lanes // TILE
    wide = lanes + TILE
    pairs = tiles // 2
    groups = rows_local // 8
    gx, gy, rep = lax.axis_index("gx"), lax.axis_index("gy"), lax.axis_index("rep")
    n_gx, n_gy, n_rep = lax.axis_size("gx"), lax.axis_size("gy"), lax.axis_size("rep")

    def present(dx, dy):
        checks = []
        if dx < 0:
            checks.append(gx > 0)
        if dx > 0:
            checks.append(gx < n_gx - 1)
        if dy < 0:
            checks.append(gy > 0)
        if dy > 0:
            checks.append(gy < n_gy - 1)
        found = checks[0]
        for check in checks[1:]:
            found = found & check
        return found

    loads = [
        pltpu.make_async_copy(vel_far, vel_ref, load_sem.at[0]),
        pltpu.make_async_copy(noise_far, noise_ref, load_sem.at[1]),
    ]
    for load in loads:
        load.start()
    barrier = pltpu.get_barrier_semaphore()
    expected = jnp.int32(n_rep - 1)
    for dx, dy in directions:
        there = present(dx, dy)
        expected = expected + there.astype(jnp.int32)

        @pl.when(there)
        def _():
            pl.semaphore_signal(barrier, inc=1, device_id={"gx": gx + dx, "gy": gy + dy}, device_id_type=MESH)

    for hop in range(1, n_rep):
        pl.semaphore_signal(barrier, inc=1, device_id={"rep": lax.rem(rep + hop, n_rep)}, device_id_type=MESH)

    stage_ref[0] = row_of(pos_ref, 0)
    stage_ref[1] = row_of(pos_ref, rows_local - 1)

    def halo_place(dx, dy):
        side = 0 if dx > 0 else 1
        if dx == 0:
            source = pos_ref.at[:, :, pl.ds(lanes - TILE if dy > 0 else 0, TILE)]
            return source, col_ref.at[0 if dy > 0 else 1]
        if dy == 0:
            return stage_ref.at[1 if dx > 0 else 0], row_ref.at[side, :, pl.ds(TILE, lanes)]
        source = stage_ref.at[1 if dx > 0 else 0, :, pl.ds(lanes - TILE if dy > 0 else 0, TILE)]
        return source, row_ref.at[side, :, pl.ds(0 if dy > 0 else TILE + lanes, TILE)]

    def halo_copy(k):
        dx, dy = directions[k]
        source, target = halo_place(dx, dy)
        return pltpu.make_async_remote_copy(
            src_ref=source, dst_ref=target, send_sem=halo_send.at[k], recv_sem=halo_recv.at[k],
            device_id={"gx": gx + dx, "gy": gy + dy}, device_id_type=MESH,
        )

    pl.semaphore_wait(barrier, expected)
    for k, (dx, dy) in enumerate(directions):
        @pl.when(present(dx, dy))
        def _():
            halo_copy(k).start()

    def own_row(row, carry):
        sub = iota((8, lanes), 0)
        half = lax.rem(iota((8, lanes), 1) // ATOMS, 2).astype(jnp.float32)
        expand = (iota((cols_local, lanes), 1) // ATOMS == iota((cols_local, lanes), 0)).astype(jnp.bfloat16)
        bias = jnp.dot(bond_bias(bond_ref[row]), expand, preferred_element_type=jnp.float32)
        base = row_of(pos_ref, row) - centre
        base = base + jnp.where(sub == 1, (half - 0.5) * spacing, 0.0)
        base = jnp.where(sub < 3, base, 0.0)
        base_ref[row] = base
        square = 2.0 / 3.0 - alpha * jnp.sum(base * base, axis=0, keepdims=True)
        one, two, three = split3(jnp.where(sub == 3, 1.0, jnp.where(sub == 4, square, base)))
        common_ref[row] = jnp.concatenate([one, two, three, one, two, one], axis=0).astype(jnp.bfloat16)
        for step in range(3):
            dx = step - 1
            extra = jnp.zeros((8, lanes), jnp.float32)
            if dx != 0:
                shift = jnp.broadcast_to(alpha * (2.0 * dx * spacing * base[0:1] - spacing * spacing), (8, lanes))
                one, two, three = split3(shift)
                extra = jnp.where(sub == 3, one, jnp.where(sub == 4, two, jnp.where(sub == 5, three, extra)))
                extra = jnp.where(sub < 3, -spacing * dx, extra)
            rhs_ref[row, step] = jnp.concatenate([bias[8 * step : 8 * step + 8], extra], axis=0).astype(jnp.bfloat16)
        return carry

    lax.fori_loop(0, rows_local, own_row, 0)

    for k, (dx, dy) in enumerate(directions):
        @pl.when(present(-dx, -dy))
        def _():
            halo_copy(k).wait_recv()

        @pl.when(jnp.logical_not(present(-dx, -dy)))
        def _():
            target = halo_place(dx, dy)[1]
            target[...] = jnp.zeros(target.shape, jnp.float32)

    def features(row, whole_row):
        sub = iota((8, wide), 0)
        slot = iota((8, wide), 1) // ATOMS
        base = pltpu.roll(whole_row, wide + TILE - ATOMS, 1)[:, :wide] - centre
        stacked = []
        for parity in range(2):
            role = lax.rem(slot + 2 * parity, 4)
            moved = base + jnp.where(sub == 1, (role.astype(jnp.float32) - 1.5) * spacing, 0.0)
            moved = jnp.where(sub < 3, moved, 0.0)
            square = -alpha * jnp.sum(moved * moved, axis=0, keepdims=True)
            vec = jnp.where(sub == 3, square, jnp.where(sub == 4, 1.0, 2.0 * alpha * moved))
            one, two, three = split3(vec)
            hot = jnp.where(sub == role, 1.0, 0.0)
            along = jnp.where(sub == 0, one[0:1], jnp.where(sub == 1, two[0:1], three[0:1]))
            along = jnp.where(sub < 3, along, jnp.where(sub < 6, 1.0, 0.0))
            stacked += [one, one, one, two, two, three, hot, along]
            coef_ref[row, parity] = jnp.concatenate([one, two], axis=0).astype(jnp.bfloat16)
        whole = jnp.concatenate(stacked, axis=0).astype(jnp.bfloat16)
        for t in range(wide // TILE):
            lhs_ref[row, t * TILE : (t + 1) * TILE] = whole[:, t * TILE : (t + 1) * TILE].T

    def inner_features(row, carry):
        features(row + 1, jnp.concatenate([row_of(col_ref.at[0], row), row_of(pos_ref, row), row_of(col_ref.at[1], row)], axis=1))
        return carry

    lax.fori_loop(0, rows_local, inner_features, 0)
    features(0, row_ref[0])
    features(rows_local + 1, row_ref[1])

    def weights(power):
        soft = jnp.exp2(power)
        square = soft * soft
        weight = square * square - soft
        high = weight.astype(jnp.bfloat16)
        return high, (weight - high.astype(jnp.float32)).astype(jnp.bfloat16)

    def rep_copy(hop, group, pair):
        chunk = slot_ref.at[
            rep, :, pl.ds(pl.multiple_of(group * 8, 8), 8), pl.ds(pl.multiple_of(pair * 2 * TILE, 2 * TILE), 2 * TILE)
        ]
        return pltpu.make_async_remote_copy(
            src_ref=chunk, dst_ref=chunk,
            send_sem=rep_send.at[hop - 1, group * pairs + pair], recv_sem=rep_recv.at[hop - 1, group * pairs + pair],
            device_id={"rep": lax.rem(rep + hop, n_rep)}, device_id_type=MESH,
        )

    def tile_rows(row, place, start, parity):
        lanes_at = pl.ds(start, TILE)
        shifts = [jnp.where(iota((8, TILE), 0) == 0, (step - 1) * spacing, 0.0) for step in range(3)]
        bases = [base_ref[row + r, :, lanes_at] for r in range(2)]
        totals = [jnp.zeros((8, TILE), jnp.float32) for _ in range(2)]

        def feat(r, step):
            block = jnp.concatenate([common_ref[row + r, :, lanes_at], rhs_ref[row + r, step, :, lanes_at]], axis=0)
            none = jnp.zeros_like(block)
            return jnp.concatenate([block, none] if parity == 0 else [none, block], axis=0)

        lhs = [lhs_ref[row + q, pl.ds(start, 2 * TILE)] for q in range(4)]
        edge = jnp.dot(
            jnp.concatenate([lhs[0], lhs[3]], axis=0),
            jnp.concatenate([feat(0, 0), feat(1, 2)], axis=1),
            preferred_element_type=jnp.float32,
        )
        blank = jnp.zeros_like(lhs[1])
        middle = jnp.dot(
            jnp.concatenate([jnp.concatenate([lhs[1], blank], axis=1), jnp.concatenate([blank, lhs[2]], axis=1)], axis=0),
            jnp.concatenate(
                [
                    jnp.concatenate([feat(0, 1), feat(1, 0)], axis=1),
                    jnp.concatenate([feat(0, 2), feat(1, 1)], axis=1),
                ],
                axis=0,
            ),
            preferred_element_type=jnp.float32,
        )
        powers = [edge[: 2 * TILE, :TILE], middle[: 2 * TILE], middle[2 * TILE :], edge[2 * TILE :, TILE:]]
        for q in range(4):
            coef = coef_ref[row + q, parity, :, pl.ds(start, 2 * TILE)]
            served = [(r, q - r) for r in range(2) if 0 <= q - r < 3]
            high, low = weights(powers[q])
            if len(served) == 1:
                sums = jnp.dot(coef, jnp.concatenate([high, low], axis=1), preferred_element_type=jnp.float32)
                sums = sums[:, :TILE] + sums[:, TILE:]
            else:
                sums = jnp.dot(coef, high, preferred_element_type=jnp.float32)
                sums = sums + jnp.dot(coef, low, preferred_element_type=jnp.float32)
            sums = sums[0:8] + sums[8:16]
            for at, (r, step) in enumerate(served):
                part = sums[:, at * TILE : (at + 1) * TILE]
                totals[r] = totals[r] + (bases[r] - shifts[step]) * part[4:5] - (0.5 / alpha) * part
        for r in range(2):
            hold_ref[place + r, :, parity * TILE : (parity + 1) * TILE] = (0.5 * ratio) * totals[r]

    def chunk_step(at, carry):
        group, pair = at // pairs, lax.rem(at, pairs)

        def row_pair(inner, unused):
            for parity in range(2):
                start = pl.multiple_of((2 * pair + parity) * TILE, TILE)
                tile_rows(group * 8 + inner * 2, inner * 2, start, parity)
            return unused

        lax.fori_loop(0, 4, row_pair, 0)
        sub = iota((8, 2 * TILE), 0)
        for d in range(3):
            block = jnp.zeros((8, 2 * TILE), jnp.float32)
            for r in range(8):
                block = jnp.where(sub == r, hold_ref[r, d : d + 1], block)
            slot_ref[
                rep, d, pl.ds(pl.multiple_of(group * 8, 8), 8), pl.ds(pl.multiple_of(pair * 2 * TILE, 2 * TILE), 2 * TILE)
            ] = block
        for hop in range(1, n_rep):
            rep_copy(hop, group, pair).start()
        return carry

    lax.fori_loop(0, groups * pairs, chunk_step, 0)

    for load in loads:
        load.wait()

    def finish(at, carry):
        group, pair = at // pairs, lax.rem(at, pairs)
        for hop in range(1, n_rep):
            chunk = slot_ref.at[
                lax.rem(rep + n_rep - hop, n_rep), :,
                pl.ds(pl.multiple_of(group * 8, 8), 8), pl.ds(pl.multiple_of(pair * 2 * TILE, 2 * TILE), 2 * TILE),
            ]
            pltpu.make_async_remote_copy(
                src_ref=chunk, dst_ref=chunk,
                send_sem=rep_send.at[hop - 1, at], recv_sem=rep_recv.at[hop - 1, at],
                device_id={"rep": lax.rem(rep + hop, n_rep)}, device_id_type=MESH,
            ).wait_recv()
        rows_at = pl.ds(pl.multiple_of(group * 8, 8), 8)
        lanes_at = pl.ds(pl.multiple_of(pair * 2 * TILE, 2 * TILE), 2 * TILE)
        total = slot_ref[0, :, rows_at, lanes_at]
        for other in range(1, n_rep):
            total = total + slot_ref[other, :, rows_at, lanes_at]
        mean = total / n_rep
        velocity = friction * vel_ref[:, rows_at, lanes_at] + time_step * mean + noise_coef * noise_ref[:, rows_at, lanes_at]
        mean_ref[:, rows_at, lanes_at] = mean
        new_vel_ref[:, rows_at, lanes_at] = velocity
        new_pos_ref[:, rows_at, lanes_at] = pos_ref[:, rows_at, lanes_at] + time_step * velocity
        for hop in range(1, n_rep):
            rep_copy(hop, group, pair).wait_send()
        return carry

    lax.fori_loop(0, groups * pairs, finish, 0)
    for k, (dx, dy) in enumerate(directions):
        @pl.when(present(dx, dy))
        def _():
            halo_copy(k).wait_send()


def per_device(positions, velocities, noise, bonds):
    _, _, rows_local, lanes = positions.shape
    n_rep = lax.axis_size("rep")
    chunks = (rows_local // 8) * (lanes // (2 * TILE))
    wide = lanes + TILE
    plane = jax.ShapeDtypeStruct((3, rows_local, lanes), jnp.float32)
    vmem = pl.BlockSpec(memory_space=pltpu.VMEM)
    mean, velocity, position = pl.pallas_call(
        step_kernel,
        out_shape=[plane] * 3,
        in_specs=[vmem, pl.BlockSpec(memory_space=pl.ANY), pl.BlockSpec(memory_space=pl.ANY), vmem],
        out_specs=[vmem] * 3,
        scratch_shapes=[
            pltpu.VMEM((rows_local + 2, wide, TILE), jnp.bfloat16),
            pltpu.VMEM((rows_local + 2, 2, 16, wide), jnp.bfloat16),
            pltpu.VMEM((rows_local, 48, lanes), jnp.bfloat16),
            pltpu.VMEM((rows_local, 3, 16, lanes), jnp.bfloat16),
            pltpu.VMEM((rows_local, 8, lanes), jnp.float32),
            pltpu.VMEM((n_rep, 3, rows_local, lanes), jnp.float32),
            pltpu.VMEM((2, 8, lanes), jnp.float32),
            pltpu.VMEM((2, 8, lanes + 2 * TILE), jnp.float32),
            pltpu.VMEM((2, 3, rows_local, TILE), jnp.float32),
            pltpu.VMEM((8, 8, 2 * TILE), jnp.float32),
            pltpu.VMEM((3, rows_local, lanes), jnp.float32),
            pltpu.VMEM((3, rows_local, lanes), jnp.float32),
            pltpu.SemaphoreType.DMA((2,)),
            pltpu.SemaphoreType.DMA((8,)),
            pltpu.SemaphoreType.DMA((8,)),
            pltpu.SemaphoreType.DMA((n_rep - 1, chunks)),
            pltpu.SemaphoreType.DMA((n_rep - 1, chunks)),
        ],
        compiler_params=pltpu.CompilerParams(
            vmem_limit_bytes=56 * 1024 * 1024, collective_id=0, has_side_effects=True
        ),
        name="forces_and_step",
    )(positions[0], velocities[0], noise[0], bonds)
    return mean, velocity[None], position[None]


def solution(mesh):
    in_specs = (
        P("rep", None, "gx", "gy"),
        P("rep", None, "gx", "gy"),
        P("rep", None, "gx", "gy"),
        P("gx", "gy", None),
    )
    out_specs = (P(None, "gx", "gy"), P("rep", None, "gx", "gy"), P("rep", None, "gx", "gy"))
    return jax.shard_map(
        per_device, mesh=mesh, in_specs=in_specs, out_specs=out_specs, check_vma=False
    )
```

```python
import jax
import jax.numpy as jnp
from jax import lax
from jax.experimental import pallas as pl
from jax.experimental.pallas import tpu as pltpu
from jax.sharding import PartitionSpec as P

ATOMS = 64
TILE = 128

spacing = 4.0
friction = 0.6
noise_coef = 0.8
time_step = 0.2
centre = 2.0
alpha = 0.5 * 1.4426950408889634
ratio = 4.0 ** (-1.0 / 3.0)
blocked = -16384.0
offset_at = ((7, 6, 5), (4, -1, 0), (1, 2, 3))


def iota(shape, axis):
    return lax.broadcasted_iota(jnp.int32, shape, axis)


def split3(value):
    first = value.astype(jnp.bfloat16).astype(jnp.float32)
    rest = value - first
    second = rest.astype(jnp.bfloat16).astype(jnp.float32)
    return first, second, rest - second


directions = ((-1, -1), (-1, 0), (-1, 1), (0, -1), (0, 1), (1, -1), (1, 0), (1, 1))
MESH = pl.DeviceIdType.MESH


def row_of(ref, row):
    sub = iota((8, ref.shape[2]), 0)
    pieces = [ref[d, pl.ds(row, 1), :] for d in range(3)]
    return jnp.where(sub == 0, pieces[0], jnp.where(sub == 1, pieces[1], jnp.where(sub == 2, pieces[2], 0.0)))


def step_kernel(
    pos_ref, vel_ref, noise_ref, bias_ref,
    mean_ref, new_vel_ref, new_pos_ref,
    lhs_ref, coef_ref, rhs_ref, base_ref, slot_ref, stage_ref, row_ref, col_ref, hold_ref,
    halo_send, halo_recv, rep_send, rep_recv,
):
    _, rows_local, lanes = pos_ref.shape
    cols_local = lanes // ATOMS
    tiles = lanes // TILE
    wide = lanes + TILE
    pairs = tiles // 2
    groups = rows_local // 8
    gx, gy, rep = lax.axis_index("gx"), lax.axis_index("gy"), lax.axis_index("rep")
    n_gx, n_gy, n_rep = lax.axis_size("gx"), lax.axis_size("gy"), lax.axis_size("rep")

    def present(dx, dy):
        checks = []
        if dx < 0:
            checks.append(gx > 0)
        if dx > 0:
            checks.append(gx < n_gx - 1)
        if dy < 0:
            checks.append(gy > 0)
        if dy > 0:
            checks.append(gy < n_gy - 1)
        found = checks[0]
        for check in checks[1:]:
            found = found & check
        return found

    barrier = pltpu.get_barrier_semaphore()
    expected = jnp.int32(n_rep - 1)
    for dx, dy in directions:
        there = present(dx, dy)
        expected = expected + there.astype(jnp.int32)

        @pl.when(there)
        def _():
            pl.semaphore_signal(barrier, inc=1, device_id={"gx": gx + dx, "gy": gy + dy}, device_id_type=MESH)

    for hop in range(1, n_rep):
        pl.semaphore_signal(barrier, inc=1, device_id={"rep": lax.rem(rep + hop, n_rep)}, device_id_type=MESH)

    stage_ref[0] = row_of(pos_ref, 0)
    stage_ref[1] = row_of(pos_ref, rows_local - 1)

    def halo_place(dx, dy):
        side = 0 if dx > 0 else 1
        if dx == 0:
            source = pos_ref.at[:, :, pl.ds(lanes - TILE if dy > 0 else 0, TILE)]
            return source, col_ref.at[0 if dy > 0 else 1]
        if dy == 0:
            return stage_ref.at[1 if dx > 0 else 0], row_ref.at[side, :, pl.ds(TILE, lanes)]
        source = stage_ref.at[1 if dx > 0 else 0, :, pl.ds(lanes - TILE if dy > 0 else 0, TILE)]
        return source, row_ref.at[side, :, pl.ds(0 if dy > 0 else TILE + lanes, TILE)]

    def halo_copy(k):
        dx, dy = directions[k]
        source, target = halo_place(dx, dy)
        return pltpu.make_async_remote_copy(
            src_ref=source, dst_ref=target, send_sem=halo_send.at[k], recv_sem=halo_recv.at[k],
            device_id={"gx": gx + dx, "gy": gy + dy}, device_id_type=MESH,
        )

    pl.semaphore_wait(barrier, expected)
    for k, (dx, dy) in enumerate(directions):
        @pl.when(present(dx, dy))
        def _():
            halo_copy(k).start()

    def own_row(row, carry):
        sub = iota((8, lanes), 0)
        half = lax.rem(iota((8, lanes), 1) // ATOMS, 2).astype(jnp.float32)
        expand = (iota((cols_local, lanes), 1) // ATOMS == iota((cols_local, lanes), 0)).astype(jnp.bfloat16)
        bias = jnp.dot(bias_ref[row].astype(jnp.bfloat16), expand, preferred_element_type=jnp.float32)
        base = row_of(pos_ref, row) - centre
        base = base + jnp.where(sub == 1, (half - 0.5) * spacing, 0.0)
        base_ref[row] = base
        for step in range(3):
            moved = base - jnp.where(sub == 0, (step - 1) * spacing, 0.0)
            moved = jnp.where(sub < 3, moved, 0.0)
            square = 2.0 / 3.0 - alpha * jnp.sum(moved * moved, axis=0, keepdims=True)
            vec = jnp.where(sub == 3, 1.0, jnp.where(sub == 4, square, 2.0 * alpha * moved))
            one, two, three = split3(vec)
            flags = bias[8 * step : 8 * step + 8]
            rhs_ref[row, step] = jnp.concatenate(
                [one, two, three, one, two, one, flags, jnp.zeros_like(flags)], axis=0
            ).astype(jnp.bfloat16)
        return carry

    lax.fori_loop(0, rows_local, own_row, 0)

    for k, (dx, dy) in enumerate(directions):
        @pl.when(present(-dx, -dy))
        def _():
            halo_copy(k).wait_recv()

        @pl.when(jnp.logical_not(present(-dx, -dy)))
        def _():
            target = halo_place(dx, dy)[1]
            target[...] = jnp.zeros(target.shape, jnp.float32)

    def features(row, whole_row):
        sub = iota((8, wide), 0)
        slot = iota((8, wide), 1) // ATOMS
        base = pltpu.roll(whole_row, wide + TILE - ATOMS, 1)[:, :wide] - centre
        stacked = []
        for parity in range(2):
            role = lax.rem(slot + 2 * parity, 4)
            moved = base + jnp.where(sub == 1, (role.astype(jnp.float32) - 1.5) * spacing, 0.0)
            moved = jnp.where(sub < 3, moved, 0.0)
            square = -alpha * jnp.sum(moved * moved, axis=0, keepdims=True)
            vec = jnp.where(sub == 3, square, jnp.where(sub == 4, 1.0, moved))
            one, two, three = split3(vec)
            hot = jnp.where(sub == role, 1.0, 0.0)
            stacked += [one, one, one, two, two, three, hot, jnp.zeros_like(hot)]
            coef_ref[row, parity] = jnp.concatenate([one, two], axis=0).astype(jnp.bfloat16)
        whole = jnp.concatenate(stacked, axis=0)
        for t in range(wide // TILE):
            lhs_ref[row, t * TILE : (t + 1) * TILE] = whole[:, t * TILE : (t + 1) * TILE].T.astype(jnp.bfloat16)

    def inner_features(row, carry):
        features(row + 1, jnp.concatenate([row_of(col_ref.at[0], row), row_of(pos_ref, row), row_of(col_ref.at[1], row)], axis=1))
        return carry

    lax.fori_loop(0, rows_local, inner_features, 0)
    features(0, row_ref[0])
    features(rows_local + 1, row_ref[1])

    def weights(lhs, rhs):
        soft = jnp.exp2(jnp.dot(lhs, rhs, preferred_element_type=jnp.float32))
        square = soft * soft
        weight = square * square - soft
        high = weight.astype(jnp.bfloat16)
        return high, (weight - high.astype(jnp.float32)).astype(jnp.bfloat16)

    def rep_copy(hop, group, pair):
        chunk = slot_ref.at[
            rep, :, pl.ds(pl.multiple_of(group * 8, 8), 8), pl.ds(pl.multiple_of(pair * 2 * TILE, 2 * TILE), 2 * TILE)
        ]
        return pltpu.make_async_remote_copy(
            src_ref=chunk, dst_ref=chunk,
            send_sem=rep_send.at[hop - 1, group * pairs + pair], recv_sem=rep_recv.at[hop - 1, group * pairs + pair],
            device_id={"rep": lax.rem(rep + hop, n_rep)}, device_id_type=MESH,
        )

    def tile_rows(row, place, start, parity):
        lanes_at = pl.ds(start, TILE)
        shifts = [jnp.where(iota((8, TILE), 0) == 0, (step - 1) * spacing, 0.0) for step in range(3)]
        bases = [base_ref[row + r, :, lanes_at] for r in range(2)]
        totals = [jnp.zeros((8, TILE), jnp.float32) for _ in range(2)]

        def feat(r, step):
            block = rhs_ref[row + r, step, :, lanes_at]
            none = jnp.zeros_like(block)
            return jnp.concatenate([block, none] if parity == 0 else [none, block], axis=0)

        for q in range(4):
            lhs = lhs_ref[row + q, pl.ds(start, 2 * TILE)]
            coef = coef_ref[row + q, parity, :, pl.ds(start, 2 * TILE)]
            served = [(r, q - r) for r in range(2) if 0 <= q - r < 3]
            rhs = jnp.concatenate([feat(r, step) for r, step in served], axis=1)
            high, low = weights(lhs, rhs)
            if len(served) == 1:
                sums = jnp.dot(coef, jnp.concatenate([high, low], axis=1), preferred_element_type=jnp.float32)
                sums = sums[:, :TILE] + sums[:, TILE:]
            else:
                sums = jnp.dot(coef, high, preferred_element_type=jnp.float32)
                sums = sums + jnp.dot(coef, low, preferred_element_type=jnp.float32)
            sums = sums[0:8] + sums[8:16]
            for at, (r, step) in enumerate(served):
                part = sums[:, at * TILE : (at + 1) * TILE]
                totals[r] = totals[r] + (bases[r] - shifts[step]) * part[4:5] - part
        for r in range(2):
            hold_ref[place + r, :, parity * TILE : (parity + 1) * TILE] = (0.5 * ratio) * totals[r]

    def chunk_step(at, carry):
        group, pair = at // pairs, lax.rem(at, pairs)

        def row_pair(inner, unused):
            for parity in range(2):
                start = pl.multiple_of((2 * pair + parity) * TILE, TILE)
                tile_rows(group * 8 + inner * 2, inner * 2, start, parity)
            return unused

        lax.fori_loop(0, 4, row_pair, 0, unroll=2)
        sub = iota((8, 2 * TILE), 0)
        for d in range(3):
            block = jnp.zeros((8, 2 * TILE), jnp.float32)
            for r in range(8):
                block = jnp.where(sub == r, hold_ref[r, d : d + 1], block)
            slot_ref[
                rep, d, pl.ds(pl.multiple_of(group * 8, 8), 8), pl.ds(pl.multiple_of(pair * 2 * TILE, 2 * TILE), 2 * TILE)
            ] = block
        for hop in range(1, n_rep):
            rep_copy(hop, group, pair).start()
        return carry

    lax.fori_loop(0, groups * pairs, chunk_step, 0)

    def finish(at, carry):
        group, pair = at // pairs, lax.rem(at, pairs)
        for hop in range(1, n_rep):
            chunk = slot_ref.at[
                lax.rem(rep + n_rep - hop, n_rep), :,
                pl.ds(pl.multiple_of(group * 8, 8), 8), pl.ds(pl.multiple_of(pair * 2 * TILE, 2 * TILE), 2 * TILE),
            ]
            pltpu.make_async_remote_copy(
                src_ref=chunk, dst_ref=chunk,
                send_sem=rep_send.at[hop - 1, at], recv_sem=rep_recv.at[hop - 1, at],
                device_id={"rep": lax.rem(rep + hop, n_rep)}, device_id_type=MESH,
            ).wait_recv()
        rows_at = pl.ds(pl.multiple_of(group * 8, 8), 8)
        lanes_at = pl.ds(pl.multiple_of(pair * 2 * TILE, 2 * TILE), 2 * TILE)
        total = slot_ref[0, :, rows_at, lanes_at]
        for other in range(1, n_rep):
            total = total + slot_ref[other, :, rows_at, lanes_at]
        mean = total / n_rep
        velocity = friction * vel_ref[:, rows_at, lanes_at] + time_step * mean + noise_coef * noise_ref[:, rows_at, lanes_at]
        mean_ref[:, rows_at, lanes_at] = mean
        new_vel_ref[:, rows_at, lanes_at] = velocity
        new_pos_ref[:, rows_at, lanes_at] = pos_ref[:, rows_at, lanes_at] + time_step * velocity
        for hop in range(1, n_rep):
            rep_copy(hop, group, pair).wait_send()
        return carry

    lax.fori_loop(0, groups * pairs, finish, 0)
    for k, (dx, dy) in enumerate(directions):
        @pl.when(present(dx, dy))
        def _():
            halo_copy(k).wait_send()


def per_device(positions, velocities, noise, bonds):
    _, _, rows_local, lanes = positions.shape
    n_rep = lax.axis_size("rep")
    chunks = (rows_local // 8) * (lanes // (2 * TILE))
    wide = lanes + TILE
    plane = jax.ShapeDtypeStruct((3, rows_local, lanes), jnp.float32)
    vmem = pl.BlockSpec(memory_space=pltpu.VMEM)
    mean, velocity, position = pl.pallas_call(
        step_kernel,
        out_shape=[plane] * 3,
        in_specs=[vmem] * 4,
        out_specs=[vmem] * 3,
        scratch_shapes=[
            pltpu.VMEM((rows_local + 2, wide, TILE), jnp.bfloat16),
            pltpu.VMEM((rows_local + 2, 2, 16, wide), jnp.bfloat16),
            pltpu.VMEM((rows_local, 3, 64, lanes), jnp.bfloat16),
            pltpu.VMEM((rows_local, 8, lanes), jnp.float32),
            pltpu.VMEM((n_rep, 3, rows_local, lanes), jnp.float32),
            pltpu.VMEM((2, 8, lanes), jnp.float32),
            pltpu.VMEM((2, 8, lanes + 2 * TILE), jnp.float32),
            pltpu.VMEM((2, 3, rows_local, TILE), jnp.float32),
            pltpu.VMEM((8, 8, 2 * TILE), jnp.float32),
            pltpu.SemaphoreType.DMA((8,)),
            pltpu.SemaphoreType.DMA((8,)),
            pltpu.SemaphoreType.DMA((n_rep - 1, chunks)),
            pltpu.SemaphoreType.DMA((n_rep - 1, chunks)),
        ],
        compiler_params=pltpu.CompilerParams(
            vmem_limit_bytes=48 * 1024 * 1024, collective_id=0, has_side_effects=True
        ),
        name="forces_and_step",
    )(positions[0], velocities[0], noise[0], bond_bias(bonds))
    return mean, velocity[None], position[None]


def bond_bias(bonds):
    cols_local = bonds.shape[1]
    odd = (jnp.arange(cols_local) % 2 == 1)[None, :]
    rows = []
    for step in range(3):
        flags = [
            jnp.ones(bonds.shape[:2], bonds.dtype) if k < 0 else bonds[:, :, k] for k in offset_at[step]
        ]
        none = jnp.zeros_like(flags[0])
        for role in range(8):
            even_flag = flags[role] if role < 3 else none
            odd_flag = flags[role - 1] if 1 <= role < 4 else none
            rows.append(jnp.where(odd, odd_flag, even_flag))
    picked = jnp.stack(rows, axis=1)
    return jnp.where(picked != 0, 0.0, blocked).astype(jnp.float32)


def solution(mesh):
    in_specs = (
        P("rep", None, "gx", "gy"),
        P("rep", None, "gx", "gy"),
        P("rep", None, "gx", "gy"),
        P("gx", "gy", None),
    )
    out_specs = (P(None, "gx", "gy"), P("rep", None, "gx", "gy"), P("rep", None, "gx", "gy"))
    return jax.shard_map(
        per_device, mesh=mesh, in_specs=in_specs, out_specs=out_specs, check_vma=False
    )
```
